128 devices in a mesh: section: 4 (over z), dp: 32 (over y, x, core).
Axes of the slice: x: 4, y: 4, z: 4, core: 2. Of those that a mesh axis runs over, the one named last changes fastest.
Arguments:
- h_saved: bfloat16 [2, 4, 128, 8, 19, 384], P(None, 'section', 'dp'), may hold values from -6 to 6
- out_cot: bfloat16 [128, 8, 19, 384], P('dp'), may hold values from -6 to 6
- so2_weight: bfloat16 [2, 4, 5, 384, 384], P(None, 'section'), may hold values from -0.3125 to 0.3125
- radial: bfloat16 [128, 112, 384], P('dp'), may hold values from 0.049804688 to 0.5
- edge_angle: float32 [128, 112], P('dp'), may hold values from -3.140625 to 3.140625
- edge_atoms: int32 [128, 2, 112], P('dp'), may hold values from 0 to 7, as said below
- edge_count: int32 [128], P('dp'), may hold values from 56 to 112
- atom_count: int32 [128], P('dp'), may hold values from 4 to 8
Outputs:
- in_grad: bfloat16 [128, 8, 19, 384], P('dp', 'section')
- weight_grad: float32 [2, 4, 5, 384, 384], P(None, 'section', None, 'dp')
The draws below stay inside these ranges and needn't reach their ends.
Inputs may be any that keep to these rules, and one draw needn't show every extreme that they name: `edge_atoms`: in micro-batch b both atoms of every edge slot are below atom_count[b]; slots from edge_count[b] on are padding.
All inputs are finite; a program needn't handle non-finite values.
Results may differ from the reference program's by a relative error of at most 0.015.
Values may be sent and summed in bfloat16 or wider, within the bound.
A program may use at most 128 MiB of HBM per device.

```python
import math
import jax
import jax.numpy as jnp
from jax import lax

C = 384
COEFFS = 19
VIRT = 2
MB = 4
A_DEV = 8
E_DEV = 112
BATCHES = 128
N_SECTION = 4
N_DP = 32


def shared_counts(key):
    key = jax.random.fold_in(key, 901)
    first_key, second_key = jax.random.split(key)
    total_slots = N_DP * MB
    counts = jax.random.randint(first_key, (total_slots,), A_DEV // 2, A_DEV + 1)
    full_slot = jax.random.randint(second_key, (), 0, total_slots)
    short_slot = (full_slot + 1) % total_slots
    counts = counts.at[full_slot].set(A_DEV).at[short_slot].set(A_DEV // 2)
    return (counts, full_slot)


def draw_atom_count(key, part):
    counts, full_slot = shared_counts(key)
    return counts.astype(jnp.int32)


def draw_edge_atoms(key, part):
    counts, full_slot = shared_counts(key)
    key = jax.random.fold_in(key, 7)
    endpoints = jax.random.randint(key, (N_DP * MB, 2, E_DEV), 0, counts[:, None, None])
    endpoints = endpoints.at[full_slot, 0, 0].set(A_DEV - 1).at[full_slot, 1, 0].set(0)
    return endpoints.astype(jnp.int32)


def draw_edge_count(key, part):
    key = jax.random.fold_in(key, 13)
    first_key, second_key = jax.random.split(key)
    total_slots = N_DP * MB
    counts = jax.random.randint(first_key, (total_slots,), E_DEV // 2, E_DEV + 1)
    pick_slot = jax.random.randint(second_key, (), 0, total_slots)
    short_slot = (pick_slot + 1) % total_slots
    counts = counts.at[pick_slot].set(E_DEV).at[short_slot].set(E_DEV // 2)
    return counts.astype(jnp.int32)


def block_levels(own_key, dims, pieces, least, top_value):
    loudness, own = 1.0, jax.random.fold_in(own_key, 6)
    for dim, blocks in pieces:
        draws = jnp.exp(jax.random.uniform(jax.random.fold_in(own, dim), (blocks,), jnp.float32, least / len(pieces), top_value / len(pieces)))
        loudness = loudness * jnp.repeat(draws, dims[dim] // blocks).reshape([-1 if axis == dim else 1 for axis in range(len(dims))])
    return loudness


def centred(rng, shape, scale, most, shards=(), held_as=jnp.bfloat16):
    values = scale * jax.random.normal(rng, shape, jnp.float32)
    if shards:
        values = values * block_levels(rng, shape, shards, -0.22, 0.18)
    return jnp.clip(values, -most, most).astype(held_as)


def setup_inputs(seed: int = 0) -> dict:
    streams_of = jax.random.split(jax.random.key(seed), 9)
    return {
        "h_saved": centred(streams_of[0], (VIRT, N_SECTION, BATCHES, A_DEV, COEFFS, C), 1.0, 6.0, ((1, 4), (2, 32))),
        "out_cot": centred(streams_of[1], (BATCHES, A_DEV, COEFFS, C), 1.0, 6.0, ((0, 32),)),
        "so2_weight": centred(streams_of[2], (VIRT, N_SECTION, 5, C, C), C ** -0.5, 0.3125, ((1, 4),)),
        "radial": jnp.clip(jnp.exp(math.log(0.5) - 2.306499 * jax.random.uniform(streams_of[3], (BATCHES, E_DEV, C), jnp.float32) ** block_levels(streams_of[3], (BATCHES, E_DEV, C), ((0, 32),), -0.2, 0.2)), 0.049804688, 0.5).astype(jnp.bfloat16),
        "edge_angle": jnp.clip(jax.random.uniform(streams_of[4], (BATCHES, E_DEV), jnp.float32, -3.140625, 3.140625), -3.140625, 3.140625),
        "edge_atoms": draw_edge_atoms(jax.random.fold_in(streams_of[8], 71), 0),
        "edge_count": draw_edge_count(jax.random.fold_in(streams_of[8], 71), 0),
        "atom_count": draw_atom_count(jax.random.fold_in(streams_of[8], 71), 0),
    }


def turn_tables(edge_angle):
    turn_order = jnp.array([1.0, 1.0, 1.0, 1.0, 2.0, 2.0, 2.0], jnp.float32)
    phase_angle = edge_angle[:, None] * turn_order[None, :]
    return (jnp.cos(phase_angle)[:, :, None], jnp.sin(phase_angle)[:, :, None])

def split_rows(values):
    flat_rows = values[:, 0:5]
    plus_rows = jnp.concatenate([values[:, 5:9], values[:, 13:16]], 1)
    minus_rows = jnp.concatenate([values[:, 9:13], values[:, 16:19]], 1)
    return (flat_rows, plus_rows, minus_rows)

def join_rows(flat_rows, plus_rows, minus_rows):
    return jnp.concatenate([flat_rows, plus_rows[:, :4], minus_rows[:, :4], plus_rows[:, 4:], minus_rows[:, 4:]], 1)

def channel_mix(values, weight):
    edge_slots, count_rows, channels = values.shape
    product = jnp.dot(values.reshape(edge_slots * count_rows, channels), weight, preferred_element_type=jnp.float32)
    return product.reshape(edge_slots, count_rows, channels)

def channel_mix_back(values, weight):
    edge_slots, count_rows, channels = values.shape
    product = lax.dot_general(values.reshape(edge_slots * count_rows, channels), weight, (((1,), (1,)), ((), ())), preferred_element_type=jnp.float32)
    return product.reshape(edge_slots, count_rows, channels)

def outer_sum(left_rows, right_rows):
    channels = left_rows.shape[2]
    return lax.dot_general(left_rows.reshape(-1, channels), right_rows.reshape(-1, channels), (((0,), (0,)), ((), ())), preferred_element_type=jnp.float32)

def so2_forward(flat_rows, plus_rows, minus_rows, weight):
    out_flat = channel_mix(flat_rows, weight[0])
    plus_parts, minus_parts = ([], [])
    for low_row, high_row, real_slot, imag_slot in ((0, 4, 1, 2), (4, 7, 3, 4)):
        width_rows = high_row - low_row
        pair_rows = jnp.concatenate([plus_rows[:, low_row:high_row], minus_rows[:, low_row:high_row]], 1)
        real_part = channel_mix(pair_rows, weight[real_slot])
        imag_part = channel_mix(pair_rows, weight[imag_slot])
        plus_parts.append(real_part[:, :width_rows] - imag_part[:, width_rows:])
        minus_parts.append(imag_part[:, :width_rows] + real_part[:, width_rows:])
    return (out_flat, jnp.concatenate(plus_parts, 1), jnp.concatenate(minus_parts, 1))

def so2_backward(flat_rows, plus_rows, minus_rows, grad_flat, grad_plus, grad_minus, weight):
    back_flat = channel_mix_back(grad_flat, weight[0])
    weight_grads = [outer_sum(flat_rows, grad_flat)]
    plus_parts, minus_parts = ([], [])
    for low_row, high_row, real_slot, imag_slot in ((0, 4, 1, 2), (4, 7, 3, 4)):
        width_rows = high_row - low_row
        pair_rows = jnp.concatenate([plus_rows[:, low_row:high_row], minus_rows[:, low_row:high_row]], 1)
        grad_pair = jnp.concatenate([grad_plus[:, low_row:high_row], grad_minus[:, low_row:high_row]], 1)
        grad_swap = jnp.concatenate([grad_minus[:, low_row:high_row], -grad_plus[:, low_row:high_row]], 1)
        real_back = channel_mix_back(grad_pair, weight[real_slot])
        imag_back = channel_mix_back(grad_pair, weight[imag_slot])
        plus_parts.append(real_back[:, :width_rows] + imag_back[:, width_rows:])
        minus_parts.append(real_back[:, width_rows:] - imag_back[:, :width_rows])
        weight_grads.append(outer_sum(pair_rows, grad_pair))
        weight_grads.append(outer_sum(pair_rows, grad_swap))
    return (back_flat, jnp.concatenate(plus_parts, 1), jnp.concatenate(minus_parts, 1), jnp.stack(weight_grads))

def layer_backward(features, upstream, weight, radial, edge_angle, edge_atoms, edge_count):
    edge_slots = edge_angle.shape[0]
    atom_slots, coeff_rows, channels = features.shape
    slot_ids = jnp.arange(atom_slots, dtype=jnp.int32)
    to_dst = (edge_atoms[0][:, None] == slot_ids[None, :]).astype(jnp.bfloat16)
    to_src = (edge_atoms[1][:, None] == slot_ids[None, :]).astype(jnp.bfloat16)
    valid_mask = (jnp.arange(edge_slots, dtype=jnp.int32) < edge_count).astype(jnp.float32)[:, None, None]
    edge_scale = radial.astype(jnp.float32)[:, None, :] * valid_mask
    cosine, sine_part = turn_tables(edge_angle)
    picked = jnp.dot(to_src, features.reshape(atom_slots, coeff_rows * channels), preferred_element_type=jnp.float32)
    picked = picked.astype(jnp.bfloat16).reshape(edge_slots, coeff_rows, channels)
    flat_rows, plus_in, minus_in = split_rows(picked)
    plus_rows = (cosine * plus_in + sine_part * minus_in).astype(jnp.bfloat16)
    minus_rows = (cosine * minus_in - sine_part * plus_in).astype(jnp.bfloat16)
    out_flat, out_plus, out_minus = so2_forward(flat_rows, plus_rows, minus_rows, weight)
    message = (join_rows(out_flat, out_plus, out_minus) * edge_scale).astype(jnp.bfloat16)
    summed_in = jnp.dot(to_dst.T, message.reshape(edge_slots, coeff_rows * channels), preferred_element_type=jnp.float32)
    summed_in = 0.25 * summed_in.reshape(atom_slots, coeff_rows, channels)
    gate_value = jax.nn.sigmoid(summed_in[:, 0, :])
    upper_grad = upstream.astype(jnp.float32)
    d_summed = upper_grad * gate_value[:, None, :]
    grad_gate = lax.optimization_barrier(jnp.sum(upper_grad * summed_in, axis=1)) * gate_value * (1.0 - gate_value)
    d_summed = jnp.concatenate([d_summed[:, 0:1, :] + grad_gate[:, None, :], d_summed[:, 1:, :]], 1)
    d_summed = (0.25 * d_summed).astype(jnp.bfloat16)
    d_message = jnp.dot(to_dst, d_summed.reshape(atom_slots, coeff_rows * channels), preferred_element_type=jnp.float32)
    d_conv = (d_message.reshape(edge_slots, coeff_rows, channels) * edge_scale).astype(jnp.bfloat16)
    grad_flat, grad_plus, grad_minus = split_rows(d_conv)
    back_flat, back_plus, back_minus, weight_grads = so2_backward(flat_rows, plus_rows, minus_rows, grad_flat, grad_plus, grad_minus, weight)
    picked_plus = cosine * back_plus - sine_part * back_minus
    picked_minus = sine_part * back_plus + cosine * back_minus
    d_picked = join_rows(back_flat, picked_plus, picked_minus).astype(jnp.bfloat16)
    spread = jnp.dot(to_src.T, d_picked.reshape(edge_slots, coeff_rows * channels), preferred_element_type=jnp.float32)
    downstream = (upper_grad + spread.reshape(atom_slots, coeff_rows, channels)).astype(jnp.bfloat16)
    return (downstream, weight_grads)

def reference(h_saved, out_cot, so2_weight, radial, edge_angle, edge_atoms, edge_count, atom_count):
    layer_total = VIRT * N_SECTION
    batch_total = N_DP * MB

    def backward_one(weight_grads, batch_index):
        upstream = out_cot[batch_index]
        for layer_index in range(layer_total - 1, -1, -1):
            lap_index, group_index = (layer_index // N_SECTION, layer_index % N_SECTION)
            upstream, layer_grads = layer_backward(h_saved[lap_index, group_index, batch_index], upstream, so2_weight[lap_index, group_index], radial[batch_index], edge_angle[batch_index], edge_atoms[batch_index], edge_count[batch_index])
            weight_grads = weight_grads.at[lap_index, group_index].add(layer_grads)
        live_atoms = (jnp.arange(A_DEV, dtype=jnp.int32) < atom_count[batch_index])[:, None, None]
        return (weight_grads, jnp.where(live_atoms, upstream, jnp.zeros_like(upstream)))
    start_grads = jnp.zeros((VIRT, N_SECTION, 5, C, C), jnp.float32)
    weight_grads, in_grad = lax.scan(backward_one, start_grads, jnp.arange(batch_total, dtype=jnp.int32))
    norm_scale = 1.0 / math.sqrt(batch_total * E_DEV)
    return (in_grad, weight_grads * norm_scale)
```

```python
import math

import jax
import jax.numpy as jnp
from jax import lax
from jax.sharding import PartitionSpec as P


def edge_tables(radial, edge_angle, edge_atoms, edge_count):
    batches, edges = edge_angle.shape
    atoms = 8
    ids = jnp.arange(atoms, dtype=jnp.int32)
    to_dst = (edge_atoms[:, 0, :, None] == ids).astype(jnp.float32)
    to_src = (edge_atoms[:, 1, :, None] == ids).astype(jnp.float32)
    valid = (jnp.arange(edges, dtype=jnp.int32)[None] < edge_count[:, None]).astype(jnp.float32)
    trig = jnp.stack(
        [
            jnp.ones_like(edge_angle),
            jnp.cos(edge_angle),
            jnp.sin(edge_angle),
            jnp.cos(2.0 * edge_angle),
            jnp.sin(2.0 * edge_angle),
        ],
        1,
    ) * (0.25 * valid[:, None])
    pick = trig[:, :, None, None, :] * (
        to_dst.transpose(0, 2, 1)[:, None, :, None, :] * to_src.transpose(0, 2, 1)[:, None, None, :, :]
    )
    pick_hi = pick.astype(jnp.bfloat16)
    pick_lo = (pick - pick_hi.astype(jnp.float32)).astype(jnp.bfloat16)
    both = jnp.concatenate([pick_hi, pick_lo], -1)
    twice = jnp.concatenate([radial, radial], 1)
    return jnp.einsum("btdse,bec->btdsc", both, twice, preferred_element_type=jnp.float32)


def complex_mix(rows, real, imag):
    plus, minus = rows[..., 0, :, :], rows[..., 1, :, :]
    both = jnp.concatenate(
        [jnp.concatenate([plus, -minus], -1), jnp.concatenate([minus, plus], -1)], -2
    )
    out = jnp.einsum(
        "...kc,cd->...kd", both, jnp.concatenate([real, imag], 0), preferred_element_type=jnp.float32
    )
    half = out.shape[-2] // 2
    return out[..., :half, :], out[..., half:, :]


def body(h_saved, out_cot, so2_weight, radial, edge_angle, edge_atoms, edge_count, atom_count):
    groups = lax.axis_size("section")
    group_index = lax.axis_index("section")
    batches, atoms, rows, channels = out_cot.shape
    table = edge_tables(radial, edge_angle, edge_atoms, edge_count)
    h = h_saved[:, 0].transpose(0, 1, 3, 2, 4)
    w = so2_weight[:, 0]
    spans = ((5, 9, 13, 1, 4), (13, 16, 19, 3, 3))

    def aggregate(values, forward):
        def apply(t, v):
            total = 0.0
            for n in range(atoms):
                tab = t[:, :, n] if forward else t[:, n]
                total = total + tab[:, None] * v[:, :, n : n + 1]
            return total

        parts = [apply(table[:, 0], values[:, 0:5])]
        for low, mid, high, slot, _ in spans:
            p, m = values[:, low:mid], values[:, mid:high]
            c, q = table[:, slot], table[:, slot + 1]
            if forward:
                parts += [apply(c, p) + apply(q, m), apply(c, m) - apply(q, p)]
            else:
                parts += [apply(c, p) - apply(q, m), apply(q, p) + apply(c, m)]
        return parts

    def forward(r):
        hr = h[r]
        out = [
            jnp.dot(hr[:, 0:5].reshape(-1, channels), w[r, 0], preferred_element_type=jnp.float32).reshape(
                batches, 5, atoms, channels
            )
        ]
        for low, mid, high, slot, k in spans:
            pair = hr[:, low:high].reshape(batches, 2, k * atoms, channels)
            p, m = complex_mix(pair, w[r, slot], w[r, slot + 1])
            out += [p.reshape(batches, k, atoms, channels), m.reshape(batches, k, atoms, channels)]
        return jnp.concatenate(aggregate(jnp.concatenate(out, 1), True), 1)

    summed = [forward(r) for r in range(2)]
    gates = [jax.nn.sigmoid(s[:, 0]) for s in summed]

    def backward(r, g):
        gf = g.astype(jnp.float32)
        gate = gates[r]
        d = gf * gate[:, None]
        extra = jnp.sum(gf * summed[r], 1) * gate * (1.0 - gate)
        d = jnp.concatenate([d[:, 0:1] + extra[:, None], d[:, 1:]], 1)
        parts = [x.astype(jnp.bfloat16) for x in aggregate(d, False)]
        nt = (((1,), (1,)), ((), ()))
        tn = (((0,), (0,)), ((), ()))
        hr = h[r]
        u0 = parts[0].reshape(-1, channels)
        back = [
            lax.dot_general(u0, w[r, 0], nt, preferred_element_type=jnp.float32).reshape(
                batches, 5, atoms, channels
            )
        ]
        grads = [lax.dot_general(hr[:, 0:5].reshape(-1, channels), u0, tn, preferred_element_type=jnp.float32)]
        for n, (low, mid, high, slot, k) in enumerate(spans):
            up = parts[1 + 2 * n].reshape(-1, channels)
            um = parts[2 + 2 * n].reshape(-1, channels)
            bar = jnp.concatenate([jnp.concatenate([up, um], 1), jnp.concatenate([um, -up], 1)], 0)
            wt = jnp.concatenate([w[r, slot], w[r, slot + 1]], 1)
            out = lax.dot_general(bar, wt, nt, preferred_element_type=jnp.float32)
            out = out.reshape(2, batches, k, atoms, channels)
            back += [out[0], out[1]]
            pair = jnp.concatenate(
                [hr[:, low:mid].reshape(-1, channels), hr[:, mid:high].reshape(-1, channels)], 0
            )
            dw = lax.dot_general(pair, bar, tn, preferred_element_type=jnp.float32)
            grads += [dw[:, :channels], dw[:, channels:]]
        return (gf + jnp.concatenate(back, 1)).astype(jnp.bfloat16), jnp.stack(grads)

    start = out_cot.transpose(0, 2, 1, 3)
    g = start
    weight_grads = []
    kept = []
    perm = [(i, (i - 1) % groups) for i in range(groups)]
    for lap in (1, 0):
        mine = None
        for step in range(groups):
            active = group_index == groups - 1 - step
            g, grads = lax.cond(
                active,
                lambda v: backward(lap, v),
                lambda v: (v, jnp.zeros((5, channels, channels), jnp.float32)),
                g,
            )
            mine = grads if mine is None else jnp.where(active, grads, mine)
            if not (lap == 0 and step == groups - 1):
                g = lax.ppermute(g, "section", perm)
        weight_grads.append(mine)
    norm_scale = 1.0 / math.sqrt(lax.axis_size("dp") * batches * edge_angle.shape[1])
    total = jnp.stack(weight_grads[::-1]) * norm_scale
    total = lax.psum_scatter(total, "dp", scatter_dimension=2, tiled=True)
    live = (jnp.arange(atoms, dtype=jnp.int32)[None, :] < atom_count[:, None])[:, None, :, None]
    g = jnp.where(live & (group_index == 0), g, jnp.zeros_like(g)).transpose(0, 2, 1, 3)
    share = atoms // groups
    own = lax.psum_scatter(g, "section", scatter_dimension=1, tiled=True)
    return own, total[:, None]


def solution(mesh):
    placed = (
        P(None, "section", "dp", None, None, None),
        P("dp", None, None, None),
        P(None, "section", None, None, None),
        P("dp", None, None),
        P("dp", None),
        P("dp", None, None),
        P("dp"),
        P("dp"),
    )
    return jax.shard_map(
        body,
        mesh=mesh,
        in_specs=placed,
        out_specs=(P("dp", "section", None, None), P(None, "section", None, "dp", None)),
        check_vma=False,
    )
```

```python
import functools
import math

import jax
import jax.numpy as jnp
from jax import lax
from jax.experimental import pallas as pl
from jax.experimental.pallas import tpu as pltpu
from jax.sharding import PartitionSpec as P

F32 = jnp.float32
BF16 = jnp.bfloat16
MESH = pl.DeviceIdType.MESH
LANES = 128
ROWS = 160
BLOCKS = ROWS // 8


def dot(a, b):
    return jnp.dot(a, b, preferred_element_type=F32)


def dot_nt(a, b):
    return lax.dot_general(a, b, (((1,), (1,)), ((), ())), preferred_element_type=F32)


def dot_tn(a, b):
    return lax.dot_general(a, b, (((0,), (0,)), ((), ())), preferred_element_type=F32)


def mix_atoms(table, values, lanes, back):
    flat = None
    pairs = []
    for n in range(8):
        term = table(0, n)[None] * values(1, 6, n)
        flat = term if flat is None else flat + term
    for lo, mid, hi, t in ((6, 10, 14, 1), (14, 17, 20, 3)):
        plus = minus = None
        for n in range(8):
            c, q = table(t, n)[None], table(t + 1, n)[None]
            p, m = values(lo, mid, n), values(mid, hi, n)
            if back:
                up, um = c * p - q * m, q * p + c * m
            else:
                up, um = c * p + q * m, c * m - q * p
            plus = up if plus is None else plus + up
            minus = um if minus is None else minus + um
        pairs += [plus, minus]
    return flat, pairs


def kernel(
    n_dp, scale, h, g0, w, radial, angle, atoms, ecount, acount, in_grad, wout,
    trig, tab_f, tab_b, hx, hs, x1, x2, y, summed, gates, dref, ub0, ub1, ub2,
    rbuf, obuf, fb, frx, dwf, pf, pk, prx, st, rs,
    ring_send, ring_recv, fin_send, fin_recv, pair_send, pair_recv, plane_send, plane_recv,
):
    batches, atom_slots, coeff_rows, channels = g0.shape
    edges = angle.shape[1]
    section = lax.axis_index("section")
    dp = lax.axis_index("dp")
    core = lax.rem(dp, 2)
    chip = dp // 2
    chips = n_dp // 2
    share = channels // n_dp
    packed = pk.shape[3]
    tiles = [pl.ds(LANES * j, LANES) for j in range(channels // LANES)]

    barrier = pltpu.get_barrier_semaphore()
    for off in range(1, 4):
        pl.semaphore_signal(barrier, inc=1, device_id=(lax.rem(section + off, 4), dp), device_id_type=MESH)
    pl.semaphore_signal(barrier, inc=1, device_id=(section, dp + 1 - 2 * core), device_id_type=MESH)

    def greet(off, carry):
        peer = lax.rem(chip + off, chips) * 2 + core
        pl.semaphore_signal(barrier, inc=1, device_id=(section, peer), device_id_type=MESH)
        return carry

    lax.fori_loop(1, chips, greet, 0)

    turn = jnp.concatenate([angle[...], 2.0 * angle[...]], 0)
    trig[0] = jnp.cos(turn)
    trig[1] = jnp.sin(turn)

    def make_tables(b, carry):
        dst = atoms[b, 0:1, :]
        src = atoms[b, 1:2, :]
        edge = lax.broadcasted_iota(jnp.int32, (1, edges), 1)
        live = jnp.where(edge < ecount[b], 0.25, 0.0).astype(F32)
        factors = [live]
        for m in range(2):
            for f in range(2):
                factors.append(live * trig[f, pl.ds(batches * m + b, 1), :])
        slot = lax.broadcasted_iota(jnp.int32, (64, edges), 0)
        for code, tab in ((src * 8 + dst, tab_f), (dst * 8 + src, tab_b)):
            hit = slot == code
            pick = jnp.concatenate([jnp.where(hit, f, 0.0) for f in factors], 0)
            high = pick.astype(BF16)
            low = (pick - high.astype(F32)).astype(BF16)
            rad = radial[b]
            tab[b] = (dot(high, rad) + dot(low, rad)).reshape(5, 8, 8, channels)
        return carry

    lax.fori_loop(0, batches, make_tables, 0)

    hx[:, 0:8, :] = jnp.zeros((len(tiles), 8, LANES), F32)

    def turn_in(read):
        for a in range(atom_slots):
            v = read(a).astype(F32)
            for j in range(len(tiles)):
                hx[j, pl.ds(8 + a, coeff_rows, stride=8), :] = v[:, LANES * j : LANES * (j + 1)]
        return jnp.concatenate([hx[j] for j in range(len(tiles))], 1)

    def forward(lap):
        def gather(b, carry):
            v = turn_in(lambda a: h[lap, b, a])
            hs[lap, b] = v.astype(BF16)
            for ref, lo, mid, hi in ((x1, 48, 80, 112), (x2, 112, 136, 160)):
                p, m = v[lo:mid], v[mid:hi]
                ref[b, :, 0:channels] = jnp.concatenate([p, m], 0).astype(BF16)
                ref[b, :, channels:] = jnp.concatenate([-m, p], 0).astype(BF16)
            return carry

        lax.fori_loop(0, batches, gather, 0)
        x0 = hs[lap, :, 0:48, :].reshape(batches * 48, channels)
        y[:, 0:6] = dot(x0, w[lap, 0]).reshape(batches, 6, 8, channels)
        w1 = w[lap, 1:3].reshape(2 * channels, channels)
        y[:, 6:14] = dot(x1[...].reshape(batches * 64, 2 * channels), w1).reshape(batches, 8, 8, channels)
        w2 = w[lap, 3:5].reshape(2 * channels, channels)
        y[:, 14:20] = dot(x2[...].reshape(batches * 48, 2 * channels), w2).reshape(batches, 6, 8, channels)

        def collect(b, carry):
            for lanes in tiles:
                flat, pairs = mix_atoms(
                    lambda t, n: tab_f[b, t, n, :, lanes],
                    lambda lo, hi, n: y[b, lo:hi, n : n + 1, lanes],
                    lanes,
                    False,
                )
                summed[lap, b, 1:6, :, lanes] = flat
                summed[lap, b, 6:10, :, lanes] = pairs[0]
                summed[lap, b, 10:14, :, lanes] = pairs[1]
                summed[lap, b, 14:17, :, lanes] = pairs[2]
                summed[lap, b, 17:20, :, lanes] = pairs[3]
                gates[lap, b, :, lanes] = jax.nn.sigmoid(flat[0])
            return carry

        lax.fori_loop(0, batches, collect, 0)

    def ring_copy(lap, b):
        there = jnp.where(section == 0, 0, lap)
        slot_there = there * batches + b
        return pltpu.make_async_remote_copy(
            src_ref=obuf.at[lap * batches + b],
            dst_ref=rbuf.at[slot_there],
            send_sem=ring_send.at[lap * batches + b],
            recv_sem=ring_recv.at[slot_there],
            device_id=(lax.rem(section + 3, 4), dp),
            device_id_type=MESH,
        )

    def ring_arrival(lap, b):
        slot = lap * batches + b
        return pltpu.make_async_remote_copy(
            src_ref=obuf.at[slot],
            dst_ref=rbuf.at[slot],
            send_sem=ring_send.at[slot],
            recv_sem=ring_recv.at[slot],
            device_id=(lax.rem(section + 3, 4), dp),
            device_id_type=MESH,
        )

    def final_copy(b, to):
        return pltpu.make_async_remote_copy(
            src_ref=fb.at[b, to],
            dst_ref=frx.at[b],
            send_sem=fin_send.at[b, to],
            recv_sem=fin_recv.at[b],
            device_id=(to, dp),
            device_id_type=MESH,
        )

    def backward(lap, b):
        slot = lap * batches + b

        @pl.when((section == 3) & (lap == 1))
        def _():
            rbuf[slot] = turn_in(lambda a: g0[b, a]).astype(BF16)

        @pl.when((section != 3) | (lap == 0))
        def _():
            ring_arrival(lap, b).wait_recv()

        for lanes in tiles:
            g = rbuf[slot, :, lanes].astype(F32).reshape(BLOCKS, 8, LANES)
            gate = gates[lap, b, :, lanes]
            extra = jnp.sum(g[1:] * summed[lap, b, 1:, :, lanes], 0) * gate * (1.0 - gate)
            d = g * gate[None]
            dref[:, :, lanes] = d
            dref[1, :, lanes] = d[1] + extra
        for j, lanes in enumerate(tiles):
            flat, pairs = mix_atoms(
                lambda t, n: tab_b[b, t, n, :, lanes],
                lambda lo, hi, n: dref[lo:hi, n : n + 1, lanes],
                lanes,
                True,
            )
            later = pl.ds(channels + LANES * j, LANES)
            pad = jnp.zeros((8, LANES), F32)
            ub0[lap, b, :, lanes] = jnp.concatenate([pad, flat.reshape(40, LANES)], 0).astype(BF16)
            for ref, (up, um) in ((ub1, pairs[0:2]), (ub2, pairs[2:4])):
                up = up.reshape(-1, LANES)
                um = um.reshape(-1, LANES)
                ref[lap, b, :, lanes] = jnp.concatenate([up, um], 0).astype(BF16)
                ref[lap, b, :, later] = jnp.concatenate([um, -up], 0).astype(BF16)
        w1 = jnp.concatenate([w[lap, 1], w[lap, 2]], 1)
        out = rbuf[slot, 48:112, :].astype(F32) + dot_nt(ub1[lap, b], w1)
        obuf[slot, 48:112, :] = out.astype(BF16)
        w2 = jnp.concatenate([w[lap, 3], w[lap, 4]], 1)
        out = rbuf[slot, 112:160, :].astype(F32) + dot_nt(ub2[lap, b], w2)
        obuf[slot, 112:160, :] = out.astype(BF16)
        out = rbuf[slot, 0:48, :].astype(F32) + dot_nt(ub0[lap, b], w[lap, 0])
        obuf[slot, 0:48, :] = out.astype(BF16)

        @pl.when((section != 0) | (lap == 1))
        def _():
            ring_copy(lap, b).start()

        @pl.when((section == 0) & (lap == 0))
        def _():
            for j, lanes in enumerate(tiles):
                hx[j] = obuf[slot, :, lanes].astype(F32)
            for to in range(4):
                for n in range(2):
                    atom = 2 * to + n
                    keep = jnp.where(acount[b] > atom, 1.0, 0.0).astype(F32)
                    for j, lanes in enumerate(tiles):
                        part = hx[j, pl.ds(8 + atom, coeff_rows, stride=8), :] * keep
                        fb[b, to, n, 0:coeff_rows, lanes] = part.astype(BF16)
            for to in range(1, 4):
                final_copy(b, to).start()

    def pair_copy(lap):
        return pltpu.make_async_remote_copy(
            src_ref=pk.at[lap, 1 - core],
            dst_ref=prx.at[lap],
            send_sem=pair_send.at[lap],
            recv_sem=pair_recv.at[lap],
            device_id=(section, dp + 1 - 2 * core),
            device_id_type=MESH,
        )

    def weight_term(lap):
        h0 = hs[lap, :, 0:48, :].reshape(batches * 48, channels)
        dwf[0] = dot_tn(h0, ub0[lap].reshape(batches * 48, channels))
        h1 = hs[lap, :, 48:112, :].reshape(batches * 64, channels)
        both = dot_tn(h1, ub1[lap].reshape(batches * 64, 2 * channels))
        dwf[1] = both[:, :channels]
        dwf[2] = both[:, channels:]
        h2 = hs[lap, :, 112:160, :].reshape(batches * 48, channels)
        both = dot_tn(h2, ub2[lap].reshape(batches * 48, 2 * channels))
        dwf[3] = both[:, :channels]
        dwf[4] = both[:, channels:]

        def pack(j, carry):
            for k in range(5):
                rows = dwf[k, pl.ds(pl.multiple_of(2 * share * j, 8), 2 * share), :]
                pf[0, share * k : share * (k + 1), :] = rows[:share]
                pf[1, share * k : share * (k + 1), :] = rows[share:]
            pk[lap, 0, j] = pf[0].astype(BF16)
            pk[lap, 1, j] = pf[1].astype(BF16)
            return carry

        lax.fori_loop(0, chips, pack, 0)
        pair_copy(lap).start()

    def plane_copy(lap, to):
        return pltpu.make_async_remote_copy(
            src_ref=st.at[lap, to],
            dst_ref=rs.at[lap, chip],
            send_sem=plane_send.at[lap, to],
            recv_sem=plane_recv.at[lap, chip],
            device_id=(section, to * 2 + core),
            device_id_type=MESH,
        )

    def plane_arrival(lap, source):
        return pltpu.make_async_remote_copy(
            src_ref=st.at[lap, source],
            dst_ref=rs.at[lap, source],
            send_sem=plane_send.at[lap, source],
            recv_sem=plane_recv.at[lap, source],
            device_id=(section, source * 2 + core),
            device_id_type=MESH,
        )

    def spread(lap):
        pair_copy(lap).wait_recv()

        def add(off, carry):
            j = lax.rem(chip + off, chips)
            st[lap, j] = (pk[lap, core, j].astype(F32) + prx[lap, j].astype(F32)).astype(BF16)

            @pl.when(off < chips)
            def _():
                plane_copy(lap, j).start()

            return carry

        lax.fori_loop(1, chips + 1, add, 0)

    def gather_grads(lap):
        wout[lap] = st[lap, chip].astype(F32)

        def take(off, carry):
            j = lax.rem(chip + off, chips)
            plane_arrival(lap, j).wait_recv()
            wout[lap] += rs[lap, j].astype(F32)
            return carry

        lax.fori_loop(1, chips, take, 0)
        wout[lap] = wout[lap] * scale

    pf[...] = jnp.zeros_like(pf)

    @pl.when(section == 0)
    def _():
        fb[...] = jnp.zeros_like(fb)

    forward(1)
    pl.semaphore_wait(barrier, 4 + chips - 1)

    def step(i, carry):
        lap = 1 - i // batches
        b = lax.rem(i, batches)

        @pl.when(((i == 0) & (section != 3)) | ((i == batches) & (section == 3)))
        def _():
            forward(0)

        @pl.when(i == batches)
        def _():
            weight_term(1)

        backward(lap, b)

        @pl.when(i == batches)
        def _():
            spread(1)

        return carry

    lax.fori_loop(0, 2 * batches, step, 0)
    weight_term(0)
    spread(0)
    gather_grads(1)

    @pl.when(section == 0)
    def _():
        for b in range(batches):
            in_grad[b] = fb[b, 0]
            for to in range(1, 4):
                final_copy(b, to).wait_send()

    @pl.when(section != 0)
    def _():
        for b in range(batches):
            final_copy(b, section).wait_recv()
            in_grad[b] = frx[b]

    gather_grads(0)

    def ring_left(i, carry):
        lap = 1 - i // batches

        @pl.when((section != 0) | (lap == 1))
        def _():
            ring_copy(lap, lax.rem(i, batches)).wait_send()

        return carry

    lax.fori_loop(0, 2 * batches, ring_left, 0)
    for lap in (1, 0):
        pair_copy(lap).wait_send()

        def left(off, carry):
            plane_copy(lap, lax.rem(chip + off, chips)).wait_send()
            return carry

        lax.fori_loop(1, chips, left, 0)


def body(n_dp, h_saved, out_cot, so2_weight, radial, edge_angle, edge_atoms, edge_count, atom_count):
    batches, atom_slots, coeff_rows, channels = out_cot.shape
    edges = edge_angle.shape[1]
    share = channels // n_dp
    packed = -(-5 * share // 16) * 16
    chips = n_dp // 2
    slots = 2 * batches
    scale = 1.0 / math.sqrt(n_dp * batches * edges)
    vmem = pl.BlockSpec(memory_space=pltpu.VMEM)
    smem = pl.BlockSpec(memory_space=pltpu.SMEM)
    dma = pltpu.SemaphoreType.DMA
    in_grad, wout = pl.pallas_call(
        functools.partial(kernel, n_dp, scale),
        out_shape=(
            jax.ShapeDtypeStruct((batches, 2, 32, channels), BF16),
            jax.ShapeDtypeStruct((2, packed, channels), F32),
        ),
        in_specs=[vmem] * 6 + [smem] * 2,
        out_specs=(vmem, vmem),
        scratch_shapes=[
            pltpu.VMEM((2, 2 * batches, edges), F32),
            pltpu.VMEM((batches, 5, 8, 8, channels), F32),
            pltpu.VMEM((batches, 5, 8, 8, channels), F32),
            pltpu.VMEM((channels // LANES, ROWS, LANES), F32),
            pltpu.VMEM((2, batches, ROWS, channels), BF16),
            pltpu.VMEM((batches, 64, 2 * channels), BF16),
            pltpu.VMEM((batches, 48, 2 * channels), BF16),
            pltpu.VMEM((batches, BLOCKS, 8, channels), F32),
            pltpu.VMEM((2, batches, BLOCKS, 8, channels), F32),
            pltpu.VMEM((2, batches, 8, channels), F32),
            pltpu.VMEM((BLOCKS, 8, channels), F32),
            pltpu.VMEM((2, batches, 48, channels), BF16),
            pltpu.VMEM((2, batches, 64, 2 * channels), BF16),
            pltpu.VMEM((2, batches, 48, 2 * channels), BF16),
            pltpu.VMEM((slots, ROWS, channels), BF16),
            pltpu.VMEM((slots, ROWS, channels), BF16),
            pltpu.VMEM((batches, 4, 2, 32, channels), BF16),
            pltpu.VMEM((batches, 2, 32, channels), BF16),
            pltpu.VMEM((5, channels, channels), F32),
            pltpu.VMEM((2, packed, channels), F32),
            pltpu.VMEM((2, 2, chips, packed, channels), BF16),
            pltpu.VMEM((2, chips, packed, channels), BF16),
            pltpu.VMEM((2, chips, packed, channels), BF16),
            pltpu.VMEM((2, chips, packed, channels), BF16),
            dma((slots,)),
            dma((slots,)),
            dma((batches, 4)),
            dma((batches,)),
            dma((2,)),
            dma((2,)),
            dma((2, chips)),
            dma((2, chips)),
        ],
        compiler_params=pltpu.CompilerParams(
            collective_id=0, has_side_effects=True, vmem_limit_bytes=52 * 1024 * 1024
        ),
        name="window_backward",
    )(
        h_saved[:, 0], out_cot, so2_weight[:, 0], radial, edge_angle, edge_atoms, edge_count, atom_count
    )
    in_grad = in_grad[:, :, :coeff_rows]
    wout = wout[:, : 5 * share].reshape(2, 1, 5, share, channels)
    return in_grad, wout


def solution(mesh):
    placed = (
        P(None, "section", "dp", None, None, None),
        P("dp", None, None, None),
        P(None, "section", None, None, None),
        P("dp", None, None),
        P("dp", None),
        P("dp", None, None),
        P("dp"),
        P("dp"),
    )
    return jax.shard_map(
        functools.partial(body, mesh.shape["dp"]),
        mesh=mesh,
        in_specs=placed,
        out_specs=(P("dp", "section", None, None), P(None, "section", None, "dp", None)),
        check_vma=False,
    )
```

```python
import functools
import math

import jax
import jax.numpy as jnp
from jax import lax
from jax.experimental import pallas as pl
from jax.experimental.pallas import tpu as pltpu
from jax.sharding import PartitionSpec as P

F32 = jnp.float32
BF16 = jnp.bfloat16
MESH = pl.DeviceIdType.MESH
LANES = 128
FIRST = (5, 13, 0)
COUNT = (8, 6, 5)
ROWS = (64, 48, 48)
TABLE = (1, 3, 0)
SLOTS = ((1, 2), (3, 4), (0,))
WIDE = (640, 640, 384)


def share_of(channels, n_dp):
    return channels // n_dp


def dot(a, b):
    return jnp.dot(a, b, preferred_element_type=F32)


def dot_nt(a, b):
    return lax.dot_general(a, b, (((1,), (1,)), ((), ())), preferred_element_type=F32)


def dot_tn(a, b):
    return lax.dot_general(a, b, (((0,), (0,)), ((), ())), preferred_element_type=F32)


def mix_flat(table, values):
    total = None
    for n in range(8):
        term = table(0, n)[None] * values(n)
        total = term if total is None else total + term
    return total


def mix_pair(table, t, plus_of, minus_of, back):
    plus = minus = None
    for n in range(8):
        c, q = table(t, n)[None], table(t + 1, n)[None]
        p, m = plus_of(n), minus_of(n)
        if back:
            up, um = c * p - q * m, q * p + c * m
        else:
            up, um = c * p + q * m, c * m - q * p
        plus = up if plus is None else plus + up
        minus = um if minus is None else minus + um
    return plus, minus


def kernel(
    n_dp, scale,
    h_in, g_in, w_in, radial_in, angle_in, atoms_in, ecount_in, acount_in, in_grad, wout,
    h, g0, w, radial, angle, atoms, ecount, acount,
    trig, tab_f, tab_b, hs1, hs2, hs0, y, summed, gates, sums, dref, ub1, ub2, ub0,
    rb1, rb2, rb0, ob1, ob2, ob0, fx, fb, frx, dwf,
    pk1, pk2, pk0, px1, px2, px0, st1, st2, st0, rs1, rs2, rs0,
    in_sem, ring_send, ring_recv, fin_send, fin_recv, pair_send, pair_recv, plane_send, plane_recv,
):
    hs, ub, rb, ob = (hs1, hs2, hs0), (ub1, ub2, ub0), (rb1, rb2, rb0), (ob1, ob2, ob0)
    pk, px, st, rs = (pk1, pk2, pk0), (px1, px2, px0), (st1, st2, st0), (rs1, rs2, rs0)
    batches, coeff_rows, atom_slots, channels = g0.shape
    edges = angle.shape[1]
    section = lax.axis_index("section")
    dp = lax.axis_index("dp")
    core = lax.rem(dp, 2)
    chip = dp // 2
    chips = n_dp // 2
    tiles = [pl.ds(LANES * j, LANES) for j in range(channels // LANES)]

    inputs = [
        pltpu.make_async_copy(src, dst, in_sem.at[n])
        for n, (src, dst) in enumerate(
            (
                (angle_in, angle),
                (atoms_in, atoms),
                (ecount_in, ecount),
                (radial_in, radial),
                (h_in.at[1], h.at[1]),
                (w_in.at[1], w.at[1]),
                (g_in, g0),
                (h_in.at[0], h.at[0]),
                (w_in.at[0], w.at[0]),
                (acount_in, acount),
            )
        )
    ]
    for copy in inputs:
        copy.start()

    barrier = pltpu.get_barrier_semaphore()
    for off in range(1, 4):
        pl.semaphore_signal(barrier, inc=1, device_id=(lax.rem(section + off, 4), dp), device_id_type=MESH)
    pl.semaphore_signal(barrier, inc=1, device_id=(section, dp + 1 - 2 * core), device_id_type=MESH)

    def greet(off, carry):
        peer = lax.rem(chip + off, chips) * 2 + core
        pl.semaphore_signal(barrier, inc=1, device_id=(section, peer), device_id_type=MESH)
        return carry

    lax.fori_loop(1, chips, greet, 0)

    for n in range(4):
        inputs[n].wait()
    turn = jnp.concatenate([angle[...], 2.0 * angle[...]], 0)
    trig[0] = jnp.cos(turn)
    trig[1] = jnp.sin(turn)

    def make_tables(b):
        dst = atoms[b, 0:1, :]
        src = atoms[b, 1:2, :]
        edge = lax.broadcasted_iota(jnp.int32, (1, edges), 1)
        live = jnp.where(edge < ecount[b], 0.25, 0.0).astype(F32)
        factors = [live]
        for m in range(2):
            for f in range(2):
                factors.append(live * trig[f, pl.ds(batches * m + b, 1), :])
        slot = lax.broadcasted_iota(jnp.int32, (64, edges), 0)
        for code, tab in ((src * 8 + dst, tab_f), (dst * 8 + src, tab_b)):
            hit = slot == code
            pick = jnp.concatenate([jnp.where(hit, f, 0.0) for f in factors], 0)
            high = pick.astype(BF16)
            low = (pick - high.astype(F32)).astype(BF16)
            rad = radial[b]
            tab[b] = (dot(high, rad) + dot(low, rad)).reshape(5, 8, 8, channels)

    def group_rows(v, k):
        v = v.astype(F32)
        if k == 2:
            v = jnp.concatenate([jnp.zeros((1, atom_slots, channels), F32), v], 0)
        return v.reshape(ROWS[k], channels)

    def prepare(p):
        lap = 1 - p // batches
        b = lax.rem(p, batches)

        @pl.when(p < batches)
        def _():
            make_tables(b)

        @pl.when(p == 0)
        def _():
            inputs[4].wait()
            inputs[5].wait()

        @pl.when(p == batches)
        def _():
            inputs[7].wait()
            inputs[8].wait()

        h0 = group_rows(h[lap, b, 0:5], 2).astype(BF16)
        hs0[lap, b] = h0
        y[0:6] = dot(h0, w[lap, 0]).reshape(6, 8, channels)
        for k, at in ((0, 6), (1, 14)):
            v = group_rows(h[lap, b, FIRST[k] : FIRST[k] + COUNT[k]], k)
            half = ROWS[k] // 2
            hs[k][lap, b] = v.astype(BF16)
            turned = jnp.concatenate([-v[half:], v[:half]], 0)
            pair = jnp.concatenate([v.astype(BF16), turned.astype(BF16)], 1)
            both = w[lap, SLOTS[k][0] : SLOTS[k][0] + 2].reshape(2 * channels, channels)
            y[at : at + COUNT[k]] = dot(pair, both).reshape(COUNT[k], 8, channels)
        for lanes in tiles:
            table = lambda t, n: tab_f[b, t, n, :, lanes]
            flat = mix_flat(table, lambda n: y[1:6, n : n + 1, lanes])
            summed[lap, b, 0:5, :, lanes] = flat
            gates[lap, b, :, lanes] = jax.nn.sigmoid(flat[0])
            for k, at in ((0, 6), (1, 14)):
                half = COUNT[k] // 2
                plus, minus = mix_pair(
                    table,
                    TABLE[k],
                    lambda n: y[at : at + half, n : n + 1, lanes],
                    lambda n: y[at + half : at + 2 * half, n : n + 1, lanes],
                    False,
                )
                summed[lap, b, FIRST[k] : FIRST[k] + half, :, lanes] = plus
                summed[lap, b, FIRST[k] + half : FIRST[k] + 2 * half, :, lanes] = minus

    def ring_copy(lap, b, k):
        slot = lap * batches + b
        there = jnp.where(section == 0, 0, lap) * batches + b
        return pltpu.make_async_remote_copy(
            src_ref=ob[k].at[slot],
            dst_ref=rb[k].at[there],
            send_sem=ring_send.at[k, slot],
            recv_sem=ring_recv.at[k, there],
            device_id=(lax.rem(section + 3, 4), dp),
            device_id_type=MESH,
        )

    def ring_arrival(lap, b, k):
        slot = lap * batches + b
        return pltpu.make_async_remote_copy(
            src_ref=ob[k].at[slot],
            dst_ref=rb[k].at[slot],
            send_sem=ring_send.at[k, slot],
            recv_sem=ring_recv.at[k, slot],
            device_id=(lax.rem(section + 3, 4), dp),
            device_id_type=MESH,
        )

    def final_copy(b, to):
        return pltpu.make_async_remote_copy(
            src_ref=fb.at[b, to],
            dst_ref=frx.at[b],
            send_sem=fin_send.at[b, to],
            recv_sem=fin_recv.at[b],
            device_id=(to, dp),
            device_id_type=MESH,
        )

    def unit(lap, b, k):
        slot = lap * batches + b
        count = COUNT[k]
        span = slice(FIRST[k], FIRST[k] + count)

        @pl.when((section == 3) & (lap == 1))
        def _():
            rb[k][slot] = group_rows(g0[b, span], k).astype(BF16)

        @pl.when((section != 3) | (lap == 0))
        def _():
            ring_arrival(lap, b, k).wait_recv()

        pad = ROWS[k] // 8 - count
        for lanes in tiles:
            g = rb[k][slot, :, lanes].astype(F32).reshape(ROWS[k] // 8, 8, LANES)[pad:]
            gate = gates[lap, b, :, lanes]
            partial = jnp.sum(g * summed[lap, b, span, :, lanes], 0)
            dref[0:count, :, lanes] = g * gate[None]
            if k == 0:
                sums[b, :, lanes] = partial
            elif k == 1:
                sums[b, :, lanes] += partial
            else:
                extra = (sums[b, :, lanes] + partial) * gate * (1.0 - gate)
                dref[0, :, lanes] += extra
        for j, lanes in enumerate(tiles):
            table = lambda t, n: tab_b[b, t, n, :, lanes]
            if k == 2:
                flat = mix_flat(table, lambda n: dref[0:5, n : n + 1, lanes])
                flat = jnp.concatenate([jnp.zeros((8, LANES), F32), flat.reshape(40, LANES)], 0)
                ub0[lap, b, :, lanes] = flat.astype(BF16)
            else:
                half = count // 2
                up, um = mix_pair(
                    table,
                    TABLE[k],
                    lambda n: dref[0:half, n : n + 1, lanes],
                    lambda n: dref[half : 2 * half, n : n + 1, lanes],
                    True,
                )
                up = up.reshape(-1, LANES)
                um = um.reshape(-1, LANES)
                later = pl.ds(channels + LANES * j, LANES)
                ub[k][lap, b, :, lanes] = jnp.concatenate([up, um], 0).astype(BF16)
                ub[k][lap, b, :, later] = jnp.concatenate([um, -up], 0).astype(BF16)
        if k == 2:
            weight = w[lap, 0]
        else:
            weight = jnp.concatenate([w[lap, SLOTS[k][0]], w[lap, SLOTS[k][1]]], 1)
        out = rb[k][slot].astype(F32) + dot_nt(ub[k][lap, b], weight)
        ob[k][slot] = out.astype(BF16)

        @pl.when((section != 0) | (lap == 1))
        def _():
            ring_copy(lap, b, k).start()

    def finish(b):
        for j, lanes in enumerate(tiles):
            fx[j, 0:40] = ob0[b, :, lanes].astype(F32)[8:]
            fx[j, 40:104] = ob1[b, :, lanes].astype(F32)
            fx[j, 104:152] = ob2[b, :, lanes].astype(F32)
        for to in range(4):
            for n in range(2):
                atom = 2 * to + n
                keep = jnp.where(acount[b] > atom, 1.0, 0.0).astype(F32)
                for j, lanes in enumerate(tiles):
                    part = fx[j, pl.ds(atom, coeff_rows, stride=8), :] * keep
                    fb[b, to, n, 0:coeff_rows, lanes] = part.astype(BF16)
        for to in range(1, 4):
            final_copy(b, to).start()

    def pair_copy(lap, k):
        return pltpu.make_async_remote_copy(
            src_ref=pk[k].at[lap, 1 - core],
            dst_ref=px[k].at[lap],
            send_sem=pair_send.at[k, lap],
            recv_sem=pair_recv.at[k, lap],
            device_id=(section, dp + 1 - 2 * core),
            device_id_type=MESH,
        )

    def weight_term(lap, k):
        left = hs[k][lap].reshape(batches * ROWS[k], channels)
        right = ub[k][lap].reshape(batches * ROWS[k], -1)
        grads = dot_tn(left, right)
        for n in range(len(SLOTS[k])):
            dwf[n] = grads[:, channels * n : channels * (n + 1)]
        low = lax.broadcasted_iota(jnp.int32, (8, channels), 0) < 4

        def pack(j, carry):
            t = [
                [dwf[n, pl.ds(pl.multiple_of(24 * j + 8 * i, 8), 8), :] for i in range(3)]
                for n in range(len(SLOTS[k]))
            ]
            if k == 2:
                blocks = (
                    jnp.concatenate([t[0][0], t[0][1]], 0),
                    jnp.concatenate([t[0][2], pltpu.roll(t[0][1], 4, 0)], 0),
                )
            else:
                blocks = []
                for c in range(2):
                    if c == 0:
                        mixed = jnp.where(low, t[0][1], pltpu.roll(t[1][1], 4, 0))
                    else:
                        mixed = jnp.where(low, pltpu.roll(t[0][1], 4, 0), t[1][1])
                    whole = jnp.concatenate([t[0][2 * c], t[1][2 * c]], 0)
                    last = jnp.concatenate([mixed[:, 256:], jnp.zeros((8, LANES), F32)], 1)
                    blocks.append(
                        jnp.concatenate([whole, jnp.concatenate([mixed[:, :256], last], 0)], 1)
                    )
            for c in range(2):
                pk[k][lap, c, j] = blocks[c].astype(BF16)
            return carry

        lax.fori_loop(0, chips, pack, 0)
        pair_copy(lap, k).start()

    def plane_copy(lap, k, to):
        return pltpu.make_async_remote_copy(
            src_ref=st[k].at[lap, to],
            dst_ref=rs[k].at[lap, chip],
            send_sem=plane_send.at[k, lap, to],
            recv_sem=plane_recv.at[k, lap, chip],
            device_id=(section, to * 2 + core),
            device_id_type=MESH,
        )

    def plane_arrival(lap, k, source):
        return pltpu.make_async_remote_copy(
            src_ref=st[k].at[lap, source],
            dst_ref=rs[k].at[lap, source],
            send_sem=plane_send.at[k, lap, source],
            recv_sem=plane_recv.at[k, lap, source],
            device_id=(section, source * 2 + core),
            device_id_type=MESH,
        )

    def spread(lap, k):
        pair_copy(lap, k).wait_recv()

        def add(off, carry):
            j = lax.rem(chip + off, chips)
            st[k][lap, j] = (pk[k][lap, core, j].astype(F32) + px[k][lap, j].astype(F32)).astype(BF16)

            @pl.when(off < chips)
            def _():
                plane_copy(lap, k, j).start()

            return carry

        lax.fori_loop(1, chips + 1, add, 0)

    def collect(lap, k):
        def take(off, total):
            j = lax.rem(chip + off, chips)
            plane_arrival(lap, k, j).wait_recv()
            return total + rs[k][lap, j].astype(F32)

        total = lax.fori_loop(1, chips, take, st[k][lap, chip].astype(F32)) * scale
        if k == 2:
            parts = [(0, total[0:8], total[8:12])]
        else:
            mixed = jnp.concatenate([total[0:8, channels:], total[8:16, channels : channels + LANES]], 1)
            parts = [
                (SLOTS[k][0], total[0:8, :channels], mixed[0:4]),
                (SLOTS[k][1], total[8:16, :channels], mixed[4:8]),
            ]
        for slot, whole, part in parts:

            @pl.when(core == 0)
            def _():
                wout[lap, slot, 0:8] = whole
                wout[lap, slot, 8:12] = part

            @pl.when(core == 1)
            def _():
                wout[lap, slot, 0:4] = part
                wout[lap, slot, 4:12] = whole

    @pl.when(section == 0)
    def _():
        fb[...] = jnp.zeros_like(fb)

    def prepare_range(lo, hi):
        def one(p, carry):
            prepare(p)
            return carry

        lax.fori_loop(lo, hi, one, 0)

    ahead = jnp.where(section == 3, 1, jnp.where(section == 2, batches, 2 * batches))
    prepare_range(0, ahead)
    inputs[6].wait()
    inputs[9].wait()
    pl.semaphore_wait(barrier, 4 + chips - 1)

    def run_lap(turn_index, carry):
        lap = 1 - turn_index

        def first(b, carry):
            now = jnp.where(section == 3, batches * turn_index + b, batches)
            until = jnp.where(section == 3, now + 1, batches + batches)
            late = (section == 3) & (lap == 1) & (b >= 1)
            fill = (section >= 2) & (lap == 0) & (b == 0)
            lo = jnp.where(fill, batches, now)
            hi = jnp.where(fill, 2 * batches, jnp.where(late, until, lo))
            prepare_range(lo, hi)
            unit(lap, b, 0)
            return carry

        lax.fori_loop(0, batches, first, 0)
        weight_term(lap, 0)

        def second(b, carry):
            unit(lap, b, 1)

            @pl.when(b == 1)
            def _():
                spread(lap, 0)

            return carry

        lax.fori_loop(0, batches, second, 0)
        weight_term(lap, 1)

        def third(b, carry):
            unit(lap, b, 2)

            @pl.when((section == 0) & (lap == 0))
            def _():
                finish(b)

            @pl.when(b == 1)
            def _():
                spread(lap, 1)

            return carry

        lax.fori_loop(0, batches, third, 0)
        weight_term(lap, 2)
        spread(lap, 2)
        return carry

    lax.fori_loop(0, 2, run_lap, 0)
    for lap, k in ((1, 0), (1, 1), (1, 2), (0, 0), (0, 1)):
        collect(lap, k)

    @pl.when(section == 0)
    def _():
        for b in range(batches):
            in_grad[b] = fb[b, 0]
            for to in range(1, 4):
                final_copy(b, to).wait_send()

    @pl.when(section != 0)
    def _():
        for b in range(batches):
            final_copy(b, section).wait_recv()
            in_grad[b] = frx[b]

    def ring_left(i, carry):
        lap = 1 - i // batches

        @pl.when((section != 0) | (lap == 1))
        def _():
            for k in range(3):
                ring_copy(lap, lax.rem(i, batches), k).wait_send()

        return carry

    lax.fori_loop(0, 2 * batches, ring_left, 0)
    for lap in (1, 0):
        for k in range(3):
            pair_copy(lap, k).wait_send()

            def left(off, carry):
                plane_copy(lap, k, lax.rem(chip + off, chips)).wait_send()
                return carry

            lax.fori_loop(1, chips, left, 0)
    collect(0, 2)


def body(n_dp, h_saved, out_cot, so2_weight, radial, edge_angle, edge_atoms, edge_count, atom_count):
    batches, atom_slots, coeff_rows, channels = out_cot.shape
    edges = edge_angle.shape[1]
    share = share_of(channels, n_dp)
    chips = n_dp // 2
    slots = 2 * batches
    scale = 1.0 / math.sqrt(n_dp * batches * edges)
    vmem = pl.BlockSpec(memory_space=pltpu.VMEM)
    dma = pltpu.SemaphoreType.DMA
    h = h_saved[:, 0].transpose(0, 1, 3, 2, 4)
    g0 = out_cot.transpose(0, 2, 1, 3)
    w = so2_weight[:, 0]
    args = (h, g0, w, radial, edge_angle, edge_atoms, edge_count, atom_count)
    homes = [pltpu.VMEM(a.shape, a.dtype) for a in args[:6]] + [pltpu.SMEM(a.shape, a.dtype) for a in args[6:]]
    in_grad, wout = pl.pallas_call(
        functools.partial(kernel, n_dp, scale),
        out_shape=(
            jax.ShapeDtypeStruct((batches, 2, 32, channels), BF16),
            jax.ShapeDtypeStruct((2, 5, share, channels), F32),
        ),
        in_specs=[pl.BlockSpec(memory_space=pl.ANY)] * 8,
        out_specs=(vmem, vmem),
        scratch_shapes=homes
        + [
            pltpu.VMEM((2, 2 * batches, edges), F32),
            pltpu.VMEM((batches, 5, 8, 8, channels), F32),
            pltpu.VMEM((batches, 5, 8, 8, channels), F32),
        ]
        + [pltpu.VMEM((2, batches, r, channels), BF16) for r in ROWS]
        + [
            pltpu.VMEM((20, 8, channels), F32),
            pltpu.VMEM((2, batches, coeff_rows, 8, channels), F32),
            pltpu.VMEM((2, batches, 8, channels), F32),
            pltpu.VMEM((batches, 8, channels), F32),
            pltpu.VMEM((8, 8, channels), F32),
            pltpu.VMEM((2, batches, ROWS[0], 2 * channels), BF16),
            pltpu.VMEM((2, batches, ROWS[1], 2 * channels), BF16),
            pltpu.VMEM((2, batches, ROWS[2], channels), BF16),
        ]
        + [pltpu.VMEM((slots, r, channels), BF16) for r in ROWS]
        + [pltpu.VMEM((slots, r, channels), BF16) for r in ROWS]
        + [
            pltpu.VMEM((channels // LANES, 152, LANES), F32),
            pltpu.VMEM((batches, 4, 2, 32, channels), BF16),
            pltpu.VMEM((batches, 2, 32, channels), BF16),
            pltpu.VMEM((2, channels, channels), F32),
        ]
        + [pltpu.VMEM((2, 2, chips, 16, n), BF16) for n in WIDE]
        + [pltpu.VMEM((2, chips, 16, n), BF16) for n in WIDE]
        + [pltpu.VMEM((2, chips, 16, n), BF16) for n in WIDE]
        + [pltpu.VMEM((2, chips, 16, n), BF16) for n in WIDE]
        + [
            dma((10,)),
            dma((3, slots)),
            dma((3, slots)),
            dma((batches, 4)),
            dma((batches,)),
            dma((3, 2)),
            dma((3, 2)),
            dma((3, 2, chips)),
            dma((3, 2, chips)),
        ],
        compiler_params=pltpu.CompilerParams(
            collective_id=0, has_side_effects=True, vmem_limit_bytes=60 * 1024 * 1024
        ),
        name="window_backward",
    )(*args)
    in_grad = in_grad[:, :, :coeff_rows]
    return in_grad, wout[:, None]


def solution(mesh):
    placed = (
        P(None, "section", "dp", None, None, None),
        P("dp", None, None, None),
        P(None, "section", None, None, None),
        P("dp", None, None),
        P("dp", None),
        P("dp", None, None),
        P("dp"),
        P("dp"),
    )
    return jax.shard_map(
        functools.partial(body, mesh.shape["dp"]),
        mesh=mesh,
        in_specs=placed,
        out_specs=(P("dp", "section", None, None), P(None, "section", None, "dp", None)),
        check_vma=False,
    )
```

```python
import functools
import math

import jax
import jax.numpy as jnp
from jax import lax
from jax.experimental import pallas as pl
from jax.experimental.pallas import tpu as pltpu
from jax.sharding import PartitionSpec as P

F32 = jnp.float32
BF16 = jnp.bfloat16
MESH = pl.DeviceIdType.MESH
LANES = 128
COEFFS = (
    ((5, 6, 9, 10), (7, 8, 11, 12)),
    ((13, 14, 16, 17), (15, 18)),
    ((3, 4), (0, 1, 2)),
)
UNITS = tuple((k, m) for k in range(3) for m in range(2))
UNIT_ROWS = (32, 32, 32, 16, 16, 32)
OFFSET = (0, 32, 0, 32, 0, 16)
BASE = (0, 4, 8, 12, 14, 16)
IN_Y = (0, 4, 8, 12, 14, 17)
ROWS = (64, 48, 48)
TABLE = (1, 3, 0)
SLOTS = ((1, 2), (3, 4), (0,))
WIDE = (640, 640, 384)


def share_of(channels, n_dp):
    return channels // n_dp


def dot(a, b):
    return jnp.dot(a, b, preferred_element_type=F32)


def dot_tn(a, b):
    return lax.dot_general(a, b, (((0,), (0,)), ((), ())), preferred_element_type=F32)


def mix_flat(table, values):
    total = None
    for n in range(8):
        term = table(0, n)[None] * values(n)
        total = term if total is None else total + term
    return total


def mix_pair(table, t, plus_of, minus_of, back):
    plus = minus = None
    for n in range(8):
        c, q = table(t, n)[None], table(t + 1, n)[None]
        p, m = plus_of(n), minus_of(n)
        if back:
            up, um = c * p - q * m, q * p + c * m
        else:
            up, um = c * p + q * m, c * m - q * p
        plus = up if plus is None else plus + up
        minus = um if minus is None else minus + um
    return plus, minus


def kernel(
    n_dp, scale,
    h_in, g_in, w_in, radial_in, angle_in, atoms_in, ecount_in, acount_in, in_grad, wout,
    h, g0, w, radial, angle, atoms, ecount, acount,
    wt, trig, tab_f, tab_b, hs1, hs2, hs0, y, summed, gates, sums, dref, ub1, ub2, ub0,
    rb_0, rb_1, rb_2, rb_3, rb_4, rb_5, ob, fx, fy, fb, frx, dwf,
    pk1, pk2, pk0, px1, px2, px0, st1, st2, st0, rs1, rs2, rs0,
    in_sem, ring_send, ring_recv, fin_send, fin_recv, pair_send, pair_recv, plane_send, plane_recv,
):
    hs, ub = (hs1, hs2, hs0), (ub1, ub2, ub0)
    rb = (rb_0, rb_1, rb_2, rb_3, rb_4, rb_5)
    pk, px, st, rs = (pk1, pk2, pk0), (px1, px2, px0), (st1, st2, st0), (rs1, rs2, rs0)
    batches, coeff_rows, atom_slots, channels = g0.shape
    edges = angle.shape[1]
    section = lax.axis_index("section")
    dp = lax.axis_index("dp")
    core = lax.rem(dp, 2)
    chip = dp // 2
    chips = n_dp // 2
    tiles = [pl.ds(LANES * j, LANES) for j in range(channels // LANES)]

    inputs = [
        pltpu.make_async_copy(src, dst, in_sem.at[n])
        for n, (src, dst) in enumerate(
            (
                (angle_in, angle),
                (atoms_in, atoms),
                (ecount_in, ecount),
                (radial_in, radial),
                (h_in.at[1], h.at[1]),
                (w_in.at[1], w.at[1]),
                (g_in, g0),
                (h_in.at[0], h.at[0]),
                (w_in.at[0], w.at[0]),
                (acount_in, acount),
            )
        )
    ]
    for copy in inputs:
        copy.start()

    barrier = pltpu.get_barrier_semaphore()
    for off in range(1, 4):
        pl.semaphore_signal(barrier, inc=1, device_id=(lax.rem(section + off, 4), dp), device_id_type=MESH)
    pl.semaphore_signal(barrier, inc=1, device_id=(section, dp + 1 - 2 * core), device_id_type=MESH)

    def greet(off, carry):
        peer = lax.rem(chip + off, chips) * 2 + core
        pl.semaphore_signal(barrier, inc=1, device_id=(section, peer), device_id_type=MESH)
        return carry

    lax.fori_loop(1, chips, greet, 0)

    for n in range(4):
        inputs[n].wait()
    turn = jnp.concatenate([angle[...], 2.0 * angle[...]], 0)
    trig[0] = jnp.cos(turn)
    trig[1] = jnp.sin(turn)

    def make_tables(b):
        dst = atoms[b, 0:1, :]
        src = atoms[b, 1:2, :]
        edge = lax.broadcasted_iota(jnp.int32, (1, edges), 1)
        live = jnp.where(edge < ecount[b], 0.25, 0.0).astype(F32)
        factors = [live]
        for m in range(2):
            for f in range(2):
                factors.append(live * trig[f, pl.ds(batches * m + b, 1), :])
        slot = lax.broadcasted_iota(jnp.int32, (64, edges), 0)
        for code, tab in ((src * 8 + dst, tab_f), (dst * 8 + src, tab_b)):
            hit = slot == code
            pick = jnp.concatenate([jnp.where(hit, f, 0.0) for f in factors], 0)
            high = pick.astype(BF16)
            low = (pick - high.astype(F32)).astype(BF16)
            rad = radial[b]
            tab[b] = (dot(high, rad) + dot(low, rad)).reshape(5, 8, 8, channels)

    def picked(ref, lap_or_none, b, coeffs):
        parts = []
        for k in coeffs:
            if k is None:
                parts.append(jnp.zeros((atom_slots, channels), F32))
            else:
                row = ref[b, abs(k)] if lap_or_none is None else ref[lap_or_none, b, abs(k)]
                parts.append(-row.astype(F32) if k < 0 else row.astype(F32))
        return jnp.concatenate(parts, 0)

    def turn_weights(lap):
        for n in range(5):
            wt[lap, channels * n : channels * (n + 1)] = w[lap, n].T

    def prepare(p):
        lap = 1 - p // batches
        b = lax.rem(p, batches)

        @pl.when(p < batches)
        def _():
            make_tables(b)

        @pl.when(p == 0)
        def _():
            inputs[4].wait()
            inputs[5].wait()
            turn_weights(1)
            inputs[7].wait()
            inputs[8].wait()
            turn_weights(0)

        h0 = picked(h, lap, b, COEFFS[2][0] + (None,) + COEFFS[2][1]).astype(BF16)
        hs0[lap, b] = h0
        y[14:20] = dot(h0, w[lap, 0]).reshape(6, 8, channels)
        for k, at in ((0, 0), (1, 8)):
            straight = COEFFS[k][0] + COEFFS[k][1]
            turned = []
            for coeffs in COEFFS[k]:
                half = len(coeffs) // 2
                turned += [-c for c in coeffs[half:]] + list(coeffs[:half])
            v = picked(h, lap, b, straight).astype(BF16)
            hs[k][lap, b] = v
            pair = jnp.concatenate([v, picked(h, lap, b, turned).astype(BF16)], 1)
            both = w[lap, SLOTS[k][0] : SLOTS[k][0] + 2].reshape(2 * channels, channels)
            y[at : at + len(straight)] = dot(pair, both).reshape(len(straight), 8, channels)
        for lanes in tiles:
            table = lambda t, n: tab_f[b, t, n, :, lanes]
            for u, (k, m) in enumerate(UNITS):
                count = len(COEFFS[k][m])
                at, to = IN_Y[u], BASE[u]
                if k == 2:
                    flat = mix_flat(table, lambda n: y[at : at + count, n : n + 1, lanes])
                    summed[lap, b, to : to + count, :, lanes] = flat
                    if m == 1:
                        gates[lap, b, :, lanes] = jax.nn.sigmoid(flat[0])
                    continue
                half = count // 2
                plus, minus = mix_pair(
                    table,
                    TABLE[k],
                    lambda n: y[at : at + half, n : n + 1, lanes],
                    lambda n: y[at + half : at + count, n : n + 1, lanes],
                    False,
                )
                summed[lap, b, to : to + half, :, lanes] = plus
                summed[lap, b, to + half : to + count, :, lanes] = minus

    def sent(lap, b, u):
        start = pl.multiple_of(b * sum(UNIT_ROWS) + sum(UNIT_ROWS[:u]), 16)
        return ob.at[lap, pl.ds(start, UNIT_ROWS[u])]

    def ring_copy(lap, b, k):
        there = jnp.where(section == 0, 0, lap) * batches + b
        return pltpu.make_async_remote_copy(
            src_ref=sent(lap, b, k),
            dst_ref=rb[k].at[there],
            send_sem=ring_send.at[lap],
            recv_sem=ring_recv.at[k, there],
            device_id=(lax.rem(section + 3, 4), dp),
            device_id_type=MESH,
        )

    def ring_arrival(lap, b, k):
        slot = lap * batches + b
        return pltpu.make_async_remote_copy(
            src_ref=sent(lap, b, k),
            dst_ref=rb[k].at[slot],
            send_sem=ring_send.at[lap],
            recv_sem=ring_recv.at[k, slot],
            device_id=(lax.rem(section + 3, 4), dp),
            device_id_type=MESH,
        )

    def final_copy(b, to):
        return pltpu.make_async_remote_copy(
            src_ref=fb.at[b, to],
            dst_ref=frx.at[b],
            send_sem=fin_send.at[0],
            recv_sem=fin_recv.at[b],
            device_id=(to, dp),
            device_id_type=MESH,
        )

    def unit(lap, b, u):
        slot = lap * batches + b
        k, m = UNITS[u]
        coeffs = COEFFS[k][m]
        count = len(coeffs)
        pad = UNIT_ROWS[u] // 8 - count
        span = slice(BASE[u], BASE[u] + count)
        rows = slice(OFFSET[u], OFFSET[u] + UNIT_ROWS[u])

        @pl.when((section == 3) & (lap == 1))
        def _():
            rb[u][slot] = picked(g0, None, b, (None,) * pad + coeffs).astype(BF16)

        @pl.when((section != 3) | (lap == 0))
        def _():
            ring_arrival(lap, b, u).wait_recv()

        for lanes in tiles:
            g = rb[u][slot, :, lanes].astype(F32).reshape(UNIT_ROWS[u] // 8, 8, LANES)[pad:]
            gate = gates[lap, b, :, lanes]
            partial = jnp.sum(g * summed[lap, b, span, :, lanes], 0)
            dref[0:count, :, lanes] = g * gate[None]
            if u == 0:
                sums[b, :, lanes] = partial
            elif u < len(UNITS) - 1:
                sums[b, :, lanes] += partial
            else:
                extra = (sums[b, :, lanes] + partial) * gate * (1.0 - gate)
                dref[0, :, lanes] += extra
        for j, lanes in enumerate(tiles):
            table = lambda t, n: tab_b[b, t, n, :, lanes]
            if k == 2:
                flat = mix_flat(table, lambda n: dref[0:count, n : n + 1, lanes]).reshape(8 * count, LANES)
                if pad:
                    flat = jnp.concatenate([jnp.zeros((8 * pad, LANES), F32), flat], 0)
                ub0[lap, b, rows, lanes] = flat.astype(BF16)
            else:
                half = count // 2
                up, um = mix_pair(
                    table,
                    TABLE[k],
                    lambda n: dref[0:half, n : n + 1, lanes],
                    lambda n: dref[half:count, n : n + 1, lanes],
                    True,
                )
                up = up.reshape(-1, LANES)
                um = um.reshape(-1, LANES)
                later = pl.ds(channels + LANES * j, LANES)
                ub[k][lap, b, rows, lanes] = jnp.concatenate([up, um], 0).astype(BF16)
                ub[k][lap, b, rows, later] = jnp.concatenate([um, -up], 0).astype(BF16)
        first_slot, n_slots = SLOTS[k][0], len(SLOTS[k])
        weight = wt[lap, channels * first_slot : channels * (first_slot + n_slots)]
        out = rb[u][slot].astype(F32) + dot(ub[k][lap, b, rows], weight)
        sent(lap, b, u)[...] = out.astype(BF16)

        @pl.when((section != 0) | (lap == 1))
        def _():
            ring_copy(lap, b, u).start()

    def finish(b):
        for j, lanes in enumerate(tiles):
            for u, (k, m) in enumerate(UNITS):
                coeffs = COEFFS[k][m]
                v = sent(0, b, u)[:, lanes].astype(F32)[UNIT_ROWS[u] - 8 * len(coeffs) :]
                for n, c in enumerate(coeffs):
                    fx[j, 8 * c : 8 * c + 8] = v[8 * n : 8 * n + 8]
        for to in range(4):
            for j, lanes in enumerate(tiles):
                for n in range(2):
                    atom = 2 * to + n
                    keep = jnp.where(acount[b] > atom, 1.0, 0.0).astype(F32)
                    part = fx[j, pl.ds(atom, coeff_rows, stride=8), :] * keep
                    fy[j, pl.ds(n, coeff_rows, stride=2), :] = part
                fb[b, to, :, lanes] = fy[j].astype(BF16)
        for to in range(1, 4):
            final_copy(b, to).start()

    def deliver(b, source):
        v = source.astype(F32)
        for k in range(coeff_rows):
            in_grad[b, k] = v[2 * k : 2 * k + 2].astype(BF16)

    def pair_copy(lap, k):
        return pltpu.make_async_remote_copy(
            src_ref=pk[k].at[lap, 1 - core],
            dst_ref=px[k].at[lap],
            send_sem=pair_send.at[k, lap],
            recv_sem=pair_recv.at[k, lap],
            device_id=(section, dp + 1 - 2 * core),
            device_id_type=MESH,
        )

    def weight_term(lap, k):
        left = hs[k][lap].reshape(batches * ROWS[k], channels)
        right = ub[k][lap].reshape(batches * ROWS[k], -1)
        grads = dot_tn(left, right)
        for n in range(len(SLOTS[k])):
            dwf[n] = grads[:, channels * n : channels * (n + 1)]
        low = lax.broadcasted_iota(jnp.int32, (8, channels), 0) < 4

        def pack(j, carry):
            t = [
                [dwf[n, pl.ds(pl.multiple_of(24 * j + 8 * i, 8), 8), :] for i in range(3)]
                for n in range(len(SLOTS[k]))
            ]
            if k == 2:
                blocks = (
                    jnp.concatenate([t[0][0], t[0][1]], 0),
                    jnp.concatenate([t[0][2], pltpu.roll(t[0][1], 4, 0)], 0),
                )
            else:
                blocks = []
                for c in range(2):
                    if c == 0:
                        mixed = jnp.where(low, t[0][1], pltpu.roll(t[1][1], 4, 0))
                    else:
                        mixed = jnp.where(low, pltpu.roll(t[0][1], 4, 0), t[1][1])
                    whole = jnp.concatenate([t[0][2 * c], t[1][2 * c]], 0)
                    last = jnp.concatenate([mixed[:, 256:], jnp.zeros((8, LANES), F32)], 1)
                    blocks.append(
                        jnp.concatenate([whole, jnp.concatenate([mixed[:, :256], last], 0)], 1)
                    )
            for c in range(2):
                pk[k][lap, c, j] = blocks[c].astype(BF16)
            return carry

        lax.fori_loop(0, chips, pack, 0, unroll=min(4, chips))
        pair_copy(lap, k).start()

    def plane_copy(lap, k, to):
        return pltpu.make_async_remote_copy(
            src_ref=st[k].at[lap, to],
            dst_ref=rs[k].at[lap, chip],
            send_sem=plane_send.at[k, lap],
            recv_sem=plane_recv.at[k, lap],
            device_id=(section, to * 2 + core),
            device_id_type=MESH,
        )

    def await_bytes(ref, sem):
        pltpu.make_async_copy(ref, ref, sem).wait()

    def spread(lap, k):
        pair_copy(lap, k).wait_recv()

        def add(off, carry):
            j = lax.rem(chip + off, chips)
            st[k][lap, j] = (pk[k][lap, core, j].astype(F32) + px[k][lap, j].astype(F32)).astype(BF16)
            plane_copy(lap, k, j).start()
            return carry

        lax.fori_loop(1, chips, add, 0, unroll=min(5, chips - 1))
        own = (pk[k][lap, core, chip].astype(F32) + px[k][lap, chip].astype(F32)).astype(BF16)
        rs[k][lap, chip] = own

    def collect(lap, k):
        await_bytes(rs[k].at[lap, 0 : chips - 1], plane_recv.at[k, lap])
        total = rs[k][lap, 0].astype(F32)
        for j in range(1, chips):
            total = total + rs[k][lap, j].astype(F32)
        total = total * scale
        if k == 2:
            parts = [(0, total[0:8], total[8:12])]
        else:
            mixed = jnp.concatenate([total[0:8, channels:], total[8:16, channels : channels + LANES]], 1)
            parts = [
                (SLOTS[k][0], total[0:8, :channels], mixed[0:4]),
                (SLOTS[k][1], total[8:16, :channels], mixed[4:8]),
            ]
        for slot, whole, part in parts:

            @pl.when(core == 0)
            def _():
                for n in range(8):
                    wout[lap, slot, n] = whole[n : n + 1]
                for n in range(4):
                    wout[lap, slot, 8 + n] = part[n : n + 1]

            @pl.when(core == 1)
            def _():
                for n in range(4):
                    wout[lap, slot, n] = part[n : n + 1]
                for n in range(8):
                    wout[lap, slot, 4 + n] = whole[n : n + 1]

    fy[...] = jnp.zeros_like(fy)

    def prepare_range(lo, hi):
        def one(p, carry):
            prepare(p)
            return carry

        lax.fori_loop(lo, hi, one, 0)

    ahead = jnp.where(section == 3, 2, jnp.where(section == 2, batches, 2 * batches))
    prepare_range(0, ahead)
    inputs[6].wait()
    inputs[9].wait()
    pl.semaphore_wait(barrier, 4 + chips - 1)

    def run_lap(turn_index, carry):
        lap = 1 - turn_index

        def first(b, carry):
            now = jnp.where(section == 3, batches * turn_index + b, batches)
            until = jnp.where(section == 3, now + 1, batches + batches)
            late = (section == 3) & (lap == 1) & (b >= 2)
            fill = (section >= 2) & (lap == 0) & (b == 0)
            lo = jnp.where(fill, batches, now)
            hi = jnp.where(fill, 2 * batches, jnp.where(late, until, lo))
            prepare_range(lo, hi)
            unit(lap, b, 0)
            unit(lap, b, 1)
            return carry

        lax.fori_loop(0, batches, first, 0)
        weight_term(lap, 0)

        def second(b, carry):
            unit(lap, b, 2)
            unit(lap, b, 3)

            @pl.when(b == 1)
            def _():
                spread(lap, 0)

            return carry

        lax.fori_loop(0, batches, second, 0)
        weight_term(lap, 1)

        def third(b, carry):
            unit(lap, b, 4)
            unit(lap, b, 5)

            @pl.when((section == 0) & (lap == 0) & (b < batches - 1))
            def _():
                finish(b)

            @pl.when(b == 1)
            def _():
                spread(lap, 1)

            return carry

        lax.fori_loop(0, batches, third, 0)
        weight_term(lap, 2)

        @pl.when((section == 0) & (lap == 0))
        def _():
            finish(batches - 1)

        spread(lap, 2)
        return carry

    lax.fori_loop(0, 2, run_lap, 0)
    for lap, k in ((1, 0), (1, 1), (1, 2), (0, 0), (0, 1)):
        collect(lap, k)


    @pl.when(section == 0)
    def _():
        for b in range(batches):
            deliver(b, fb[b, 0])
        await_bytes(fb.at[0:3], fin_send.at[0])

    await_bytes(ob.at[1], ring_send.at[1])

    @pl.when(section != 0)
    def _():
        await_bytes(ob.at[0], ring_send.at[0])

    for lap in (1, 0):
        for k in range(3):
            pair_copy(lap, k).wait_send()
            await_bytes(st[k].at[lap, 0 : chips - 1], plane_send.at[k, lap])

    collect(0, 2)

    @pl.when(section != 0)
    def _():
        for b in range(batches):
            final_copy(b, section).wait_recv()
            deliver(b, frx[b])


def body(n_dp, h_saved, out_cot, so2_weight, radial, edge_angle, edge_atoms, edge_count, atom_count):
    batches, atom_slots, coeff_rows, channels = out_cot.shape
    edges = edge_angle.shape[1]
    share = share_of(channels, n_dp)
    chips = n_dp // 2
    slots = 2 * batches
    scale = 1.0 / math.sqrt(n_dp * batches * edges)
    vmem = pl.BlockSpec(memory_space=pltpu.VMEM)
    dma = pltpu.SemaphoreType.DMA
    h = h_saved[:, 0].transpose(0, 1, 3, 2, 4)
    g0 = out_cot.transpose(0, 2, 1, 3)
    w = so2_weight[:, 0]
    args = (h, g0, w, radial, edge_angle, edge_atoms, edge_count, atom_count)
    homes = [pltpu.VMEM(a.shape, a.dtype) for a in args[:6]] + [pltpu.SMEM(a.shape, a.dtype) for a in args[6:]]
    in_grad, wout = pl.pallas_call(
        functools.partial(kernel, n_dp, scale),
        out_shape=(
            pltpu.VMEM((batches, coeff_rows, 2, channels), BF16),
            pltpu.VMEM((2, 5, share, 1, channels), F32),
        ),
        in_specs=[pl.BlockSpec(memory_space=pl.ANY)] * 8,
        out_specs=(vmem, vmem),
        scratch_shapes=homes
        + [
            pltpu.VMEM((2, 5 * channels, channels), BF16),
            pltpu.VMEM((2, 2 * batches, edges), F32),
            pltpu.VMEM((batches, 5, 8, 8, channels), F32),
            pltpu.VMEM((batches, 5, 8, 8, channels), F32),
        ]
        + [pltpu.VMEM((2, batches, r, channels), BF16) for r in ROWS]
        + [
            pltpu.VMEM((20, 8, channels), F32),
            pltpu.VMEM((2, batches, coeff_rows, 8, channels), F32),
            pltpu.VMEM((2, batches, 8, channels), F32),
            pltpu.VMEM((batches, 8, channels), F32),
            pltpu.VMEM((8, 8, channels), F32),
            pltpu.VMEM((2, batches, ROWS[0], 2 * channels), BF16),
            pltpu.VMEM((2, batches, ROWS[1], 2 * channels), BF16),
            pltpu.VMEM((2, batches, ROWS[2], channels), BF16),
        ]
        + [pltpu.VMEM((slots, r, channels), BF16) for r in UNIT_ROWS]
        + [
            pltpu.VMEM((2, batches * sum(UNIT_ROWS), channels), BF16),
            pltpu.VMEM((channels // LANES, 152, LANES), F32),
            pltpu.VMEM((channels // LANES, 48, LANES), F32),
            pltpu.VMEM((batches, 4, 48, channels), BF16),
            pltpu.VMEM((batches, 48, channels), BF16),
            pltpu.VMEM((2, channels, channels), F32),
        ]
        + [pltpu.VMEM((2, 2, chips, 16, n), BF16) for n in WIDE]
        + [pltpu.VMEM((2, chips, 16, n), BF16) for n in WIDE]
        + [pltpu.VMEM((2, chips, 16, n), BF16) for n in WIDE]
        + [pltpu.VMEM((2, chips, 16, n), BF16) for n in WIDE]
        + [
            dma((10,)),
            dma((2,)),
            dma((len(UNITS), slots)),
            dma((1,)),
            dma((batches,)),
            dma((3, 2)),
            dma((3, 2)),
            dma((3, 2)),
            dma((3, 2)),
        ],
        compiler_params=pltpu.CompilerParams(
            collective_id=0, has_side_effects=True, vmem_limit_bytes=60 * 1024 * 1024
        ),
        name="window_backward",
    )(*args)
    return in_grad.transpose(0, 2, 1, 3), wout.transpose(0, 3, 1, 2, 4)


def solution(mesh):
    placed = (
        P(None, "section", "dp", None, None, None),
        P("dp", None, None, None),
        P(None, "section", None, None, None),
        P("dp", None, None),
        P("dp", None),
        P("dp", None, None),
        P("dp"),
        P("dp"),
    )
    return jax.shard_map(
        functools.partial(body, mesh.shape["dp"]),
        mesh=mesh,
        in_specs=placed,
        out_specs=(P("dp", "section", None, None), P(None, "section", None, "dp", None)),
        check_vma=False,
    )
```

```python
import functools
import math

import jax
import jax.numpy as jnp
from jax import lax
from jax.experimental import pallas as pl
from jax.experimental.pallas import tpu as pltpu
from jax.sharding import PartitionSpec as P

F32 = jnp.float32
BF16 = jnp.bfloat16
MESH = pl.DeviceIdType.MESH
LANES = 128
COEFFS = (
    ((5, 6, 9, 10), (7, 8, 11, 12)),
    ((13, 14, 16, 17), (15, 18)),
    ((3, 4), (0, 1, 2)),
)
UNITS = tuple((k, m) for k in range(3) for m in range(2))
UNIT_ROWS = (32, 32, 32, 16, 16, 32)
OFFSET = (0, 32, 0, 32, 0, 16)
BASE = (0, 4, 8, 12, 14, 16)
IN_Y = (0, 4, 8, 12, 14, 17)
ROWS = (64, 48, 48)
TABLE = (1, 3, 0)
SLOTS = ((1, 2), (3, 4), (0,))
WIDE = (640, 640, 384)


def share_of(channels, n_dp):
    return channels // n_dp


def dot(a, b):
    return jnp.dot(a, b, preferred_element_type=F32)


def dot_tn(a, b):
    return lax.dot_general(a, b, (((0,), (0,)), ((), ())), preferred_element_type=F32)


def mix_flat(table, values):
    total = None
    for n in range(8):
        term = table(0, n)[None] * values(n)
        total = term if total is None else total + term
    return total


def mix_pair(table, t, plus_of, minus_of, back):
    plus = minus = None
    for n in range(8):
        c, q = table(t, n)[None], table(t + 1, n)[None]
        p, m = plus_of(n), minus_of(n)
        if back:
            up, um = c * p - q * m, q * p + c * m
        else:
            up, um = c * p + q * m, c * m - q * p
        plus = up if plus is None else plus + up
        minus = um if minus is None else minus + um
    return plus, minus


def kernel(
    n_dp, scale,
    h_in, g_in, w_in, radial_in, angle_in, atoms_in, ecount_in, acount_in, in_grad, wout,
    h, g0, w, radial, angle, atoms, ecount, acount,
    wt, trig, tab_f, tab_b, hs1, hs2, hs0, y, summed, gates, sums, dref, ub1, ub2, ub0,
    rb_0, rb_1, rb_2, rb_3, rb_4, rb_5, ob, fx, fy, fb, frx, dwf,
    hx1, hx2, hx0, ux1, ux2, ux0, pk1, pk2, pk0, rs1, rs2, rs0,
    in_sem, ring_send, ring_recv, fin_send, fin_recv, pair_send, pair_recv, plane_send, plane_recv,
):
    hs, ub = (hs1, hs2, hs0), (ub1, ub2, ub0)
    rb = (rb_0, rb_1, rb_2, rb_3, rb_4, rb_5)
    hx, ux = (hx1, hx2, hx0), (ux1, ux2, ux0)
    pk, rs = (pk1, pk2, pk0), (rs1, rs2, rs0)
    batches, coeff_rows, atom_slots, channels = g0.shape
    edges = angle.shape[1]
    section = lax.axis_index("section")
    dp = lax.axis_index("dp")
    core = lax.rem(dp, 2)
    chip = dp // 2
    chips = n_dp // 2
    tiles = [pl.ds(LANES * j, LANES) for j in range(channels // LANES)]

    inputs = [
        pltpu.make_async_copy(src, dst, in_sem.at[n])
        for n, (src, dst) in enumerate(
            (
                (angle_in, angle),
                (atoms_in, atoms),
                (ecount_in, ecount),
                (radial_in, radial),
                (h_in.at[1], h.at[1]),
                (w_in.at[1], w.at[1]),
                (g_in, g0),
                (h_in.at[0], h.at[0]),
                (w_in.at[0], w.at[0]),
                (acount_in, acount),
            )
        )
    ]
    for copy in inputs:
        copy.start()

    barrier = pltpu.get_barrier_semaphore()
    for off in range(1, 4):
        pl.semaphore_signal(barrier, inc=1, device_id=(lax.rem(section + off, 4), dp), device_id_type=MESH)
    pl.semaphore_signal(barrier, inc=1, device_id=(section, dp + 1 - 2 * core), device_id_type=MESH)

    def greet(off, carry):
        peer = lax.rem(chip + off, chips) * 2 + core
        pl.semaphore_signal(barrier, inc=1, device_id=(section, peer), device_id_type=MESH)
        return carry

    lax.fori_loop(1, chips, greet, 0)

    for n in range(4):
        inputs[n].wait()
    turn = jnp.concatenate([angle[...], 2.0 * angle[...]], 0)
    trig[0] = jnp.cos(turn)
    trig[1] = jnp.sin(turn)

    def make_tables(b):
        dst = atoms[b, 0:1, :]
        src = atoms[b, 1:2, :]
        edge = lax.broadcasted_iota(jnp.int32, (1, edges), 1)
        live = jnp.where(edge < ecount[b], 0.25, 0.0).astype(F32)
        factors = [live]
        for m in range(2):
            for f in range(2):
                factors.append(live * trig[f, pl.ds(batches * m + b, 1), :])
        slot = lax.broadcasted_iota(jnp.int32, (64, edges), 0)
        for code, tab in ((src * 8 + dst, tab_f), (dst * 8 + src, tab_b)):
            hit = slot == code
            pick = jnp.concatenate([jnp.where(hit, f, 0.0) for f in factors], 0)
            high = pick.astype(BF16)
            low = (pick - high.astype(F32)).astype(BF16)
            rad = radial[b]
            tab[b] = (dot(high, rad) + dot(low, rad)).reshape(5, 8, 8, channels)

    def picked(ref, lap_or_none, b, coeffs):
        parts = []
        for k in coeffs:
            if k is None:
                parts.append(jnp.zeros((atom_slots, channels), F32))
            else:
                row = ref[b, abs(k)] if lap_or_none is None else ref[lap_or_none, b, abs(k)]
                parts.append(-row.astype(F32) if k < 0 else row.astype(F32))
        return jnp.concatenate(parts, 0)

    def turn_weights(lap, slots):
        for n in slots:
            wt[lap, channels * n : channels * (n + 1)] = w[lap, n].T

    def prepare(p):
        lap = 1 - p // batches
        b = lax.rem(p, batches)

        @pl.when(p < batches)
        def _():
            make_tables(b)

        @pl.when(p == 0)
        def _():
            inputs[4].wait()
            inputs[5].wait()
            turn_weights(1, (1, 2))

        h0 = picked(h, lap, b, COEFFS[2][0] + (None,) + COEFFS[2][1]).astype(BF16)
        hs0[lap, b] = h0
        y[14:20] = dot(h0, w[lap, 0]).reshape(6, 8, channels)
        for k, at in ((0, 0), (1, 8)):
            straight = COEFFS[k][0] + COEFFS[k][1]
            turned = []
            for coeffs in COEFFS[k]:
                half = len(coeffs) // 2
                turned += [-c for c in coeffs[half:]] + list(coeffs[:half])
            v = picked(h, lap, b, straight).astype(BF16)
            hs[k][lap, b] = v
            pair = jnp.concatenate([v, picked(h, lap, b, turned).astype(BF16)], 1)
            both = w[lap, SLOTS[k][0] : SLOTS[k][0] + 2].reshape(2 * channels, channels)
            y[at : at + len(straight)] = dot(pair, both).reshape(len(straight), 8, channels)
        for lanes in tiles:
            table = lambda t, n: tab_f[b, t, n, :, lanes]
            for u, (k, m) in enumerate(UNITS):
                count = len(COEFFS[k][m])
                at, to = IN_Y[u], BASE[u]
                if k == 2:
                    flat = mix_flat(table, lambda n: y[at : at + count, n : n + 1, lanes])
                    summed[lap, b, to : to + count, :, lanes] = flat
                    if m == 1:
                        gates[lap, b, :, lanes] = jax.nn.sigmoid(flat[0])
                    continue
                half = count // 2
                plus, minus = mix_pair(
                    table,
                    TABLE[k],
                    lambda n: y[at : at + half, n : n + 1, lanes],
                    lambda n: y[at + half : at + count, n : n + 1, lanes],
                    False,
                )
                summed[lap, b, to : to + half, :, lanes] = plus
                summed[lap, b, to + half : to + count, :, lanes] = minus

    def sent(lap, b, u):
        start = pl.multiple_of(b * sum(UNIT_ROWS) + sum(UNIT_ROWS[:u]), 16)
        return ob.at[lap, pl.ds(start, UNIT_ROWS[u])]

    def ring_copy(lap, b, k):
        there = jnp.where(section == 0, 0, lap) * batches + b
        return pltpu.make_async_remote_copy(
            src_ref=sent(lap, b, k),
            dst_ref=rb[k].at[there],
            send_sem=ring_send.at[lap],
            recv_sem=ring_recv.at[k, there],
            device_id=(lax.rem(section + 3, 4), dp),
            device_id_type=MESH,
        )

    def ring_arrival(lap, b, k):
        slot = lap * batches + b
        return pltpu.make_async_remote_copy(
            src_ref=sent(lap, b, k),
            dst_ref=rb[k].at[slot],
            send_sem=ring_send.at[lap],
            recv_sem=ring_recv.at[k, slot],
            device_id=(lax.rem(section + 3, 4), dp),
            device_id_type=MESH,
        )

    def final_copy(b, to):
        return pltpu.make_async_remote_copy(
            src_ref=fb.at[b, to],
            dst_ref=frx.at[b],
            send_sem=fin_send.at[0],
            recv_sem=fin_recv.at[b],
            device_id=(to, dp),
            device_id_type=MESH,
        )

    def unit(lap, b, u):
        slot = lap * batches + b
        k, m = UNITS[u]
        coeffs = COEFFS[k][m]
        count = len(coeffs)
        pad = UNIT_ROWS[u] // 8 - count
        span = slice(BASE[u], BASE[u] + count)
        rows = slice(OFFSET[u], OFFSET[u] + UNIT_ROWS[u])

        @pl.when((section == 3) & (lap == 1))
        def _():
            rb[u][slot] = picked(g0, None, b, (None,) * pad + coeffs).astype(BF16)

        @pl.when((section != 3) | (lap == 0))
        def _():
            ring_arrival(lap, b, u).wait_recv()

        for lanes in tiles:
            g = rb[u][slot, :, lanes].astype(F32).reshape(UNIT_ROWS[u] // 8, 8, LANES)[pad:]
            gate = gates[lap, b, :, lanes]
            partial = jnp.sum(g * summed[lap, b, span, :, lanes], 0)
            dref[0:count, :, lanes] = g * gate[None]
            if u == 0:
                sums[b, :, lanes] = partial
            elif u < len(UNITS) - 1:
                sums[b, :, lanes] += partial
            else:
                extra = (sums[b, :, lanes] + partial) * gate * (1.0 - gate)
                dref[0, :, lanes] += extra
        for j, lanes in enumerate(tiles):
            table = lambda t, n: tab_b[b, t, n, :, lanes]
            if k == 2:
                flat = mix_flat(table, lambda n: dref[0:count, n : n + 1, lanes]).reshape(8 * count, LANES)
                if pad:
                    flat = jnp.concatenate([jnp.zeros((8 * pad, LANES), F32), flat], 0)
                ub0[lap, b, rows, lanes] = flat.astype(BF16)
            else:
                half = count // 2
                up, um = mix_pair(
                    table,
                    TABLE[k],
                    lambda n: dref[0:half, n : n + 1, lanes],
                    lambda n: dref[half:count, n : n + 1, lanes],
                    True,
                )
                up = up.reshape(-1, LANES)
                um = um.reshape(-1, LANES)
                later = pl.ds(channels + LANES * j, LANES)
                ub[k][lap, b, rows, lanes] = jnp.concatenate([up, um], 0).astype(BF16)
                ub[k][lap, b, rows, later] = jnp.concatenate([um, -up], 0).astype(BF16)
        if m == 1:
            for copy in pair_copies(lap, b, k):
                copy.start()
        first_slot, n_slots = SLOTS[k][0], len(SLOTS[k])
        weight = wt[lap, channels * first_slot : channels * (first_slot + n_slots)]
        out = rb[u][slot].astype(F32) + dot(ub[k][lap, b, rows], weight)
        sent(lap, b, u)[...] = out.astype(BF16)

        @pl.when((section != 0) | (lap == 1))
        def _():
            ring_copy(lap, b, u).start()

    def finish(b):
        for j, lanes in enumerate(tiles):
            for u, (k, m) in enumerate(UNITS):
                coeffs = COEFFS[k][m]
                v = sent(0, b, u)[:, lanes].astype(F32)[UNIT_ROWS[u] - 8 * len(coeffs) :]
                for n, c in enumerate(coeffs):
                    fx[j, 8 * c : 8 * c + 8] = v[8 * n : 8 * n + 8]
        for to in range(4):
            for j, lanes in enumerate(tiles):
                for n in range(2):
                    atom = 2 * to + n
                    keep = jnp.where(acount[b] > atom, 1.0, 0.0).astype(F32)
                    part = fx[j, pl.ds(atom, coeff_rows, stride=8), :] * keep
                    fy[j, pl.ds(n, coeff_rows, stride=2), :] = part
                fb[b, to, :, lanes] = fy[j].astype(BF16)
        for to in range(1, 4):
            final_copy(b, to).start()

    def deliver(b, source):
        v = source.astype(F32)
        for k in range(coeff_rows):
            in_grad[b, k] = v[2 * k : 2 * k + 2].astype(BF16)

    def pair_copies(lap, b, k):
        return [
            pltpu.make_async_remote_copy(
                src_ref=src[k].at[lap, b],
                dst_ref=dst[k].at[lap, b],
                send_sem=pair_send.at[n, k, lap],
                recv_sem=pair_recv.at[n, k, lap],
                device_id=(section, dp + 1 - 2 * core),
                device_id_type=MESH,
            )
            for n, (src, dst) in enumerate(((hs, hx), (ub, ux)))
        ]

    def await_bytes(ref, sem):
        pltpu.make_async_copy(ref, ref, sem).wait()

    def plane_copy(lap, k, to):
        return pltpu.make_async_remote_copy(
            src_ref=pk[k].at[lap, to],
            dst_ref=rs[k].at[lap, chip],
            send_sem=plane_send.at[k, lap],
            recv_sem=plane_recv.at[k, lap],
            device_id=(section, to * 2 + core),
            device_id_type=MESH,
        )

    def weight_term(lap, k):
        def product(left, right):
            rows = batches * ROWS[k]
            return dot_tn(left[k][lap].reshape(rows, channels), right[k][lap].reshape(rows, -1))

        grads = product(hs, ub)
        await_bytes(hx[k].at[lap], pair_recv.at[0, k, lap])
        await_bytes(ux[k].at[lap], pair_recv.at[1, k, lap])
        grads = grads + product(hx, ux)
        for n in range(len(SLOTS[k])):
            dwf[n] = grads[:, channels * n : channels * (n + 1)]
        low = lax.broadcasted_iota(jnp.int32, (8, channels), 0) < 4

        def rows_of(n, start):
            return dwf[n, pl.ds(pl.multiple_of(start, 8), 8), :]

        def block(j):
            whole = [rows_of(n, 24 * j + 16 * core) for n in range(len(SLOTS[k]))]
            middle = [rows_of(n, 24 * j + 8) for n in range(len(SLOTS[k]))]
            raised = jnp.where(core == 0, middle[0], pltpu.roll(middle[0], 4, 0))
            if k == 2:
                return jnp.concatenate([whole[0], raised], 0).astype(BF16)
            lowered = jnp.where(core == 0, pltpu.roll(middle[1], 4, 0), middle[1])
            mixed = jnp.where(low, raised, lowered)
            last = jnp.concatenate([mixed[:, 256:], jnp.zeros((8, LANES), F32)], 1)
            side = jnp.concatenate([mixed[:, :256], last], 0)
            return jnp.concatenate([jnp.concatenate(whole, 0), side], 1).astype(BF16)

        def pack(off, carry):
            j = lax.rem(chip + off, chips)
            pk[k][lap, j] = block(j)
            plane_copy(lap, k, j).start()
            return carry

        lax.fori_loop(1, chips, pack, 0, unroll=min(5, chips - 1))
        rs[k][lap, chip] = block(chip)

    def collect(lap, k):
        await_bytes(rs[k].at[lap, 0 : chips - 1], plane_recv.at[k, lap])
        total = rs[k][lap, 0].astype(F32)
        for j in range(1, chips):
            total = total + rs[k][lap, j].astype(F32)
        total = total * scale
        if k == 2:
            parts = [(0, total[0:8], total[8:12])]
        else:
            mixed = jnp.concatenate([total[0:8, channels:], total[8:16, channels : channels + LANES]], 1)
            parts = [
                (SLOTS[k][0], total[0:8, :channels], mixed[0:4]),
                (SLOTS[k][1], total[8:16, :channels], mixed[4:8]),
            ]
        for slot, whole, part in parts:

            @pl.when(core == 0)
            def _():
                for n in range(8):
                    wout[lap, slot, n] = whole[n : n + 1]
                for n in range(4):
                    wout[lap, slot, 8 + n] = part[n : n + 1]

            @pl.when(core == 1)
            def _():
                for n in range(4):
                    wout[lap, slot, n] = part[n : n + 1]
                for n in range(8):
                    wout[lap, slot, 4 + n] = whole[n : n + 1]

    fy[...] = jnp.zeros_like(fy)

    def prepare_range(lo, hi):
        def one(p, carry):
            prepare(p)
            return carry

        lax.fori_loop(lo, hi, one, 0)

    prepare_range(0, jnp.where(section == 3, 1, batches))

    def turn_rest():
        turn_weights(1, (3, 4, 0))
        inputs[7].wait()
        inputs[8].wait()
        turn_weights(0, range(5))

    @pl.when(section != 3)
    def _():
        turn_rest()

    inputs[6].wait()
    inputs[9].wait()
    pl.semaphore_wait(barrier, 4 + chips - 1)

    def run_lap(turn_index, carry):
        lap = 1 - turn_index

        def first(b, carry):
            now = jnp.where(section == 3, batches * turn_index + b, batches)
            until = jnp.where(section == 3, now + 1, batches + batches)
            late = (section == 3) & (lap == 1) & (b >= 1)
            fill = (section >= 2) & (lap == 0) & (b == 0)
            early = (section < 2) & (lap == 1) & (b == 0)
            fill = fill | early
            lo = jnp.where(fill, batches, now)
            hi = jnp.where(fill, 2 * batches, jnp.where(late, until, lo))
            prepare_range(lo, hi)
            unit(lap, b, 0)
            unit(lap, b, 1)
            return carry

        lax.fori_loop(0, batches, first, 0)

        @pl.when((section == 3) & (lap == 1))
        def _():
            turn_rest()

        now = (section != 3) | (lap == 0)

        def second(b, carry):
            unit(lap, b, 2)
            unit(lap, b, 3)

            @pl.when((b == 1) & now)
            def _():
                weight_term(lap, 0)

            return carry

        lax.fori_loop(0, batches, second, 0)

        def third(b, carry):
            unit(lap, b, 4)
            unit(lap, b, 5)

            @pl.when((section == 0) & (lap == 0) & (b < batches - 1))
            def _():
                finish(b)

            @pl.when((b == 1) & now)
            def _():
                weight_term(lap, 1)

            return carry

        lax.fori_loop(0, batches, third, 0)

        @pl.when(now)
        def _():
            weight_term(lap, 2)

        @pl.when((section == 0) & (lap == 0))
        def _():
            finish(batches - 1)

        return carry

    lax.fori_loop(0, 2, run_lap, 0)

    @pl.when(section == 3)
    def _():
        for k in range(3):
            weight_term(1, k)

    for lap, k in ((1, 0), (1, 1), (1, 2), (0, 0), (0, 1)):
        collect(lap, k)


    @pl.when(section == 0)
    def _():
        for b in range(batches):
            deliver(b, fb[b, 0])
        await_bytes(fb.at[0:3], fin_send.at[0])

    await_bytes(ob.at[1], ring_send.at[1])

    @pl.when(section != 0)
    def _():
        await_bytes(ob.at[0], ring_send.at[0])

    for lap in (1, 0):
        for k in range(3):
            await_bytes(hs[k].at[lap], pair_send.at[0, k, lap])
            await_bytes(ub[k].at[lap], pair_send.at[1, k, lap])
            await_bytes(pk[k].at[lap, 0 : chips - 1], plane_send.at[k, lap])

    collect(0, 2)

    @pl.when(section != 0)
    def _():
        for b in range(batches):
            final_copy(b, section).wait_recv()
            deliver(b, frx[b])


def body(n_dp, h_saved, out_cot, so2_weight, radial, edge_angle, edge_atoms, edge_count, atom_count):
    batches, atom_slots, coeff_rows, channels = out_cot.shape
    edges = edge_angle.shape[1]
    share = share_of(channels, n_dp)
    chips = n_dp // 2
    slots = 2 * batches
    scale = 1.0 / math.sqrt(n_dp * batches * edges)
    vmem = pl.BlockSpec(memory_space=pltpu.VMEM)
    dma = pltpu.SemaphoreType.DMA
    h = h_saved[:, 0].transpose(0, 1, 3, 2, 4)
    g0 = out_cot.transpose(0, 2, 1, 3)
    w = so2_weight[:, 0]
    args = (h, g0, w, radial, edge_angle, edge_atoms, edge_count, atom_count)
    homes = [pltpu.VMEM(a.shape, a.dtype) for a in args[:6]] + [pltpu.SMEM(a.shape, a.dtype) for a in args[6:]]
    in_grad, wout = pl.pallas_call(
        functools.partial(kernel, n_dp, scale),
        out_shape=(
            pltpu.VMEM((batches, coeff_rows, 2, channels), BF16),
            pltpu.VMEM((2, 5, share, 1, channels), F32),
        ),
        in_specs=[pl.BlockSpec(memory_space=pl.ANY)] * 8,
        out_specs=(vmem, vmem),
        scratch_shapes=homes
        + [
            pltpu.VMEM((2, 5 * channels, channels), BF16),
            pltpu.VMEM((2, 2 * batches, edges), F32),
            pltpu.VMEM((batches, 5, 8, 8, channels), F32),
            pltpu.VMEM((batches, 5, 8, 8, channels), F32),
        ]
        + [pltpu.VMEM((2, batches, r, channels), BF16) for r in ROWS]
        + [
            pltpu.VMEM((20, 8, channels), F32),
            pltpu.VMEM((2, batches, coeff_rows, 8, channels), F32),
            pltpu.VMEM((2, batches, 8, channels), F32),
            pltpu.VMEM((batches, 8, channels), F32),
            pltpu.VMEM((8, 8, channels), F32),
            pltpu.VMEM((2, batches, ROWS[0], 2 * channels), BF16),
            pltpu.VMEM((2, batches, ROWS[1], 2 * channels), BF16),
            pltpu.VMEM((2, batches, ROWS[2], channels), BF16),
        ]
        + [pltpu.VMEM((slots, r, channels), BF16) for r in UNIT_ROWS]
        + [
            pltpu.VMEM((2, batches * sum(UNIT_ROWS), channels), BF16),
            pltpu.VMEM((channels // LANES, 152, LANES), F32),
            pltpu.VMEM((channels // LANES, 48, LANES), F32),
            pltpu.VMEM((batches, 4, 48, channels), BF16),
            pltpu.VMEM((batches, 48, channels), BF16),
            pltpu.VMEM((2, channels, channels), F32),
        ]
        + [pltpu.VMEM((2, batches, r, channels), BF16) for r in ROWS]
        + [
            pltpu.VMEM((2, batches, ROWS[0], 2 * channels), BF16),
            pltpu.VMEM((2, batches, ROWS[1], 2 * channels), BF16),
            pltpu.VMEM((2, batches, ROWS[2], channels), BF16),
        ]
        + [pltpu.VMEM((2, chips, 16, n), BF16) for n in WIDE]
        + [pltpu.VMEM((2, chips, 16, n), BF16) for n in WIDE]
        + [
            dma((10,)),
            dma((2,)),
            dma((len(UNITS), slots)),
            dma((1,)),
            dma((batches,)),
            dma((2, 3, 2)),
            dma((2, 3, 2)),
            dma((3, 2)),
            dma((3, 2)),
        ],
        compiler_params=pltpu.CompilerParams(
            collective_id=0, has_side_effects=True, vmem_limit_bytes=60 * 1024 * 1024
        ),
        name="window_backward",
    )(*args)
    return in_grad.transpose(0, 2, 1, 3), wout.transpose(0, 3, 1, 2, 4)


def solution(mesh):
    placed = (
        P(None, "section", "dp", None, None, None),
        P("dp", None, None, None),
        P(None, "section", None, None, None),
        P("dp", None, None),
        P("dp", None),
        P("dp", None, None),
        P("dp"),
        P("dp"),
    )
    return jax.shard_map(
        functools.partial(body, mesh.shape["dp"]),
        mesh=mesh,
        in_specs=placed,
        out_specs=(P("dp", "section", None, None), P(None, "section", None, "dp", None)),
        check_vma=False,
    )
```

```python
import functools
import math

import jax
import jax.numpy as jnp
from jax import lax
from jax.experimental import pallas as pl
from jax.experimental.pallas import tpu as pltpu
from jax.sharding import PartitionSpec as P

F32 = jnp.float32
BF16 = jnp.bfloat16
MESH = pl.DeviceIdType.MESH
LANES = 128
COEFFS = (
    ((5, 6, 9, 10), (7, 8, 11, 12)),
    ((13, 14, 16, 17), (15, 18)),
    ((3, 4), (0, 1, 2)),
)
UNITS = tuple((k, m) for k in range(3) for m in range(2))
UNIT_ROWS = (32, 32, 32, 16, 16, 32)
OFFSET = (0, 32, 0, 32, 0, 16)
BASE = (0, 4, 8, 12, 14, 16)
IN_Y = (0, 4, 8, 12, 14, 17)
ROWS = (64, 48, 48)
TABLE = (1, 3, 0)
SLOTS = ((1, 2), (3, 4), (0,))
WIDE = (640, 640, 384)


def share_of(channels, n_dp):
    return channels // n_dp


def dot(a, b):
    return jnp.dot(a, b, preferred_element_type=F32)


def dot_tn(a, b):
    return lax.dot_general(a, b, (((0,), (0,)), ((), ())), preferred_element_type=F32)


def mix_flat(table, values):
    total = None
    for n in range(8):
        term = table(0, n)[None] * values(n)
        total = term if total is None else total + term
    return total


def mix_pair(table, t, plus_of, minus_of, back):
    plus = minus = None
    for n in range(8):
        c, q = table(t, n)[None], table(t + 1, n)[None]
        p, m = plus_of(n), minus_of(n)
        if back:
            up, um = c * p - q * m, q * p + c * m
        else:
            up, um = c * p + q * m, c * m - q * p
        plus = up if plus is None else plus + up
        minus = um if minus is None else minus + um
    return plus, minus


def kernel(
    n_dp, scale,
    h_in, g_in, w_in, radial_in, angle_in, atoms_in, ecount_in, acount_in, in_grad, wout,
    h, g0, w, radial, angle, atoms, ecount, acount,
    wt, trig, tab_f, tab_b, hs1, hs2, hs0, y, summed, gates, sums, dref, ub1, ub2, ub0,
    rb_0, rb_1, rb_2, rb_3, rb_4, rb_5, ob, fx, fy, fb, frx, dwf,
    hx1, hx2, hx0, ux1, ux2, ux0, pk1, pk2, pk0, rs1, rs2, rs0,
    in_sem, ring_send, ring_recv, fin_send, fin_recv, pair_send, pair_recv, plane_send, plane_recv,
):
    hs, ub = (hs1, hs2, hs0), (ub1, ub2, ub0)
    rb = (rb_0, rb_1, rb_2, rb_3, rb_4, rb_5)
    hx, ux = (hx1, hx2, hx0), (ux1, ux2, ux0)
    pk, rs = (pk1, pk2, pk0), (rs1, rs2, rs0)
    batches, coeff_rows, atom_slots, channels = g0.shape
    edges = angle.shape[1]
    section = lax.axis_index("section")
    dp = lax.axis_index("dp")
    core = lax.rem(dp, 2)
    chip = dp // 2
    chips = n_dp // 2
    tiles = [pl.ds(LANES * j, LANES) for j in range(channels // LANES)]

    inputs = [
        pltpu.make_async_copy(src, dst, in_sem.at[n])
        for n, (src, dst) in enumerate(
            (
                (angle_in, angle),
                (atoms_in, atoms),
                (ecount_in, ecount),
                (radial_in, radial),
                (h_in.at[1], h.at[1]),
                (w_in.at[1], w.at[1]),
                (g_in, g0),
                (h_in.at[0], h.at[0]),
                (w_in.at[0], w.at[0]),
                (acount_in, acount),
            )
        )
    ]
    for copy in inputs:
        copy.start()

    barrier = pltpu.get_barrier_semaphore()
    for off in range(1, 4):
        pl.semaphore_signal(barrier, inc=1, device_id=(lax.rem(section + off, 4), dp), device_id_type=MESH)
    pl.semaphore_signal(barrier, inc=1, device_id=(section, dp + 1 - 2 * core), device_id_type=MESH)

    def greet(off, carry):
        peer = lax.rem(chip + off, chips) * 2 + core
        pl.semaphore_signal(barrier, inc=1, device_id=(section, peer), device_id_type=MESH)
        return carry

    lax.fori_loop(1, chips, greet, 0)

    for n in range(4):
        inputs[n].wait()
    turn = jnp.concatenate([angle[...], 2.0 * angle[...]], 0)
    trig[0] = jnp.cos(turn)
    trig[1] = jnp.sin(turn)

    def make_tables(b):
        dst = atoms[b, 0:1, :]
        src = atoms[b, 1:2, :]
        edge = lax.broadcasted_iota(jnp.int32, (1, edges), 1)
        live = jnp.where(edge < ecount[b], 0.25, 0.0).astype(F32)
        factors = [live]
        for m in range(2):
            for f in range(2):
                factors.append(live * trig[f, pl.ds(batches * m + b, 1), :])
        slot = lax.broadcasted_iota(jnp.int32, (64, edges), 0)
        for code, tab in ((src * 8 + dst, tab_f), (dst * 8 + src, tab_b)):
            hit = slot == code
            pick = jnp.concatenate([jnp.where(hit, f, 0.0) for f in factors], 0)
            high = pick.astype(BF16)
            low = (pick - high.astype(F32)).astype(BF16)
            rad = radial[b]
            tab[b] = (dot(high, rad) + dot(low, rad)).reshape(5, 8, 8, channels)

    def picked(ref, lap_or_none, b, coeffs):
        parts = []
        for k in coeffs:
            if k is None:
                parts.append(jnp.zeros((atom_slots, channels), F32))
            else:
                row = ref[b, abs(k)] if lap_or_none is None else ref[lap_or_none, b, abs(k)]
                parts.append(-row.astype(F32) if k < 0 else row.astype(F32))
        return jnp.concatenate(parts, 0)

    def turn_weights(lap, slots):
        for n in slots:
            wt[lap, channels * n : channels * (n + 1)] = w[lap, n].T

    def prepare(p):
        lap = 1 - p // batches
        b = lax.rem(p, batches)

        @pl.when(p < batches)
        def _():
            make_tables(b)

        @pl.when(p == 0)
        def _():
            inputs[4].wait()
            inputs[5].wait()
            turn_weights(1, (1, 2))

        h0 = picked(h, lap, b, COEFFS[2][0] + (None,) + COEFFS[2][1]).astype(BF16)
        hs0[lap, b] = h0
        y[14:20] = dot(h0, w[lap, 0]).reshape(6, 8, channels)
        for k, at in ((0, 0), (1, 8)):
            straight = COEFFS[k][0] + COEFFS[k][1]
            turned = []
            for coeffs in COEFFS[k]:
                half = len(coeffs) // 2
                turned += [-c for c in coeffs[half:]] + list(coeffs[:half])
            v = picked(h, lap, b, straight).astype(BF16)
            hs[k][lap, b] = v
            pair = jnp.concatenate([v, picked(h, lap, b, turned).astype(BF16)], 1)
            both = w[lap, SLOTS[k][0] : SLOTS[k][0] + 2].reshape(2 * channels, channels)
            y[at : at + len(straight)] = dot(pair, both).reshape(len(straight), 8, channels)
        for lanes in tiles:
            table = lambda t, n: tab_f[b, t, n, :, lanes]
            for u, (k, m) in enumerate(UNITS):
                count = len(COEFFS[k][m])
                at, to = IN_Y[u], BASE[u]
                if k == 2:
                    flat = mix_flat(table, lambda n: y[at : at + count, n : n + 1, lanes])
                    summed[lap, b, to : to + count, :, lanes] = flat
                    if m == 1:
                        gates[lap, b, :, lanes] = jax.nn.sigmoid(flat[0])
                    continue
                half = count // 2
                plus, minus = mix_pair(
                    table,
                    TABLE[k],
                    lambda n: y[at : at + half, n : n + 1, lanes],
                    lambda n: y[at + half : at + count, n : n + 1, lanes],
                    False,
                )
                summed[lap, b, to : to + half, :, lanes] = plus
                summed[lap, b, to + half : to + count, :, lanes] = minus

    def sent(lap, b, u):
        start = pl.multiple_of(b * sum(UNIT_ROWS) + sum(UNIT_ROWS[:u]), 16)
        return ob.at[lap, pl.ds(start, UNIT_ROWS[u])]

    def ring_copy(lap, b, k):
        there = jnp.where(section == 0, 0, lap) * batches + b
        return pltpu.make_async_remote_copy(
            src_ref=sent(lap, b, k),
            dst_ref=rb[k].at[there],
            send_sem=ring_send.at[lap],
            recv_sem=ring_recv.at[k, there],
            device_id=(lax.rem(section + 3, 4), dp),
            device_id_type=MESH,
        )

    def ring_arrival(lap, b, k):
        slot = lap * batches + b
        return pltpu.make_async_remote_copy(
            src_ref=sent(lap, b, k),
            dst_ref=rb[k].at[slot],
            send_sem=ring_send.at[lap],
            recv_sem=ring_recv.at[k, slot],
            device_id=(lax.rem(section + 3, 4), dp),
            device_id_type=MESH,
        )

    def final_copy(b, to):
        return pltpu.make_async_remote_copy(
            src_ref=fb.at[b, to],
            dst_ref=frx.at[b],
            send_sem=fin_send.at[0],
            recv_sem=fin_recv.at[b],
            device_id=(to, dp),
            device_id_type=MESH,
        )

    def unit(lap, b, u):
        slot = lap * batches + b
        k, m = UNITS[u]
        coeffs = COEFFS[k][m]
        count = len(coeffs)
        pad = UNIT_ROWS[u] // 8 - count
        span = slice(BASE[u], BASE[u] + count)
        rows = slice(OFFSET[u], OFFSET[u] + UNIT_ROWS[u])

        @pl.when((section == 3) & (lap == 1))
        def _():
            rb[u][slot] = picked(g0, None, b, (None,) * pad + coeffs).astype(BF16)

        @pl.when((section != 3) | (lap == 0))
        def _():
            ring_arrival(lap, b, u).wait_recv()

        for lanes in tiles:
            g = rb[u][slot, :, lanes].astype(F32).reshape(UNIT_ROWS[u] // 8, 8, LANES)[pad:]
            gate = gates[lap, b, :, lanes]
            partial = jnp.sum(g * summed[lap, b, span, :, lanes], 0)
            dref[0:count, :, lanes] = g * gate[None]
            if u == 0:
                sums[b, :, lanes] = partial
            elif u < len(UNITS) - 1:
                sums[b, :, lanes] += partial
            else:
                extra = (sums[b, :, lanes] + partial) * gate * (1.0 - gate)
                dref[0, :, lanes] += extra
        for j, lanes in enumerate(tiles):
            table = lambda t, n: tab_b[b, t, n, :, lanes]
            if k == 2:
                flat = mix_flat(table, lambda n: dref[0:count, n : n + 1, lanes]).reshape(8 * count, LANES)
                if pad:
                    flat = jnp.concatenate([jnp.zeros((8 * pad, LANES), F32), flat], 0)
                ub0[lap, b, rows, lanes] = flat.astype(BF16)
            else:
                half = count // 2
                up, um = mix_pair(
                    table,
                    TABLE[k],
                    lambda n: dref[0:half, n : n + 1, lanes],
                    lambda n: dref[half:count, n : n + 1, lanes],
                    True,
                )
                up = up.reshape(-1, LANES)
                um = um.reshape(-1, LANES)
                later = pl.ds(channels + LANES * j, LANES)
                ub[k][lap, b, rows, lanes] = jnp.concatenate([up, um], 0).astype(BF16)
                ub[k][lap, b, rows, later] = jnp.concatenate([um, -up], 0).astype(BF16)
        first_slot, n_slots = SLOTS[k][0], len(SLOTS[k])
        weight = wt[lap, channels * first_slot : channels * (first_slot + n_slots)]
        out = rb[u][slot].astype(F32) + dot(ub[k][lap, b, rows], weight)
        sent(lap, b, u)[...] = out.astype(BF16)

        @pl.when((section != 0) | (lap == 1))
        def _():
            ring_copy(lap, b, u).start()

        if m == 1:
            for copy in pair_copies(lap, b, k):
                copy.start()

    def finish(b):
        for j, lanes in enumerate(tiles):
            for u, (k, m) in enumerate(UNITS):
                coeffs = COEFFS[k][m]
                v = sent(0, b, u)[:, lanes].astype(F32)[UNIT_ROWS[u] - 8 * len(coeffs) :]
                for n, c in enumerate(coeffs):
                    fx[j, 8 * c : 8 * c + 8] = v[8 * n : 8 * n + 8]
        for to in range(4):
            for j, lanes in enumerate(tiles):
                for n in range(2):
                    atom = 2 * to + n
                    keep = jnp.where(acount[b] > atom, 1.0, 0.0).astype(F32)
                    part = fx[j, pl.ds(atom, coeff_rows, stride=8), :] * keep
                    fy[j, pl.ds(n, coeff_rows, stride=2), :] = part
                fb[b, to, :, lanes] = fy[j].astype(BF16)
        for to in range(1, 4):
            final_copy(b, to).start()

    def deliver(b, source):
        v = source.astype(F32)
        for k in range(coeff_rows):
            in_grad[b, k] = v[2 * k : 2 * k + 2].astype(BF16)

    def pair_copies(lap, b, k):
        return [
            pltpu.make_async_remote_copy(
                src_ref=src[k].at[lap, b],
                dst_ref=dst[k].at[lap, b],
                send_sem=pair_send.at[n, k, lap],
                recv_sem=pair_recv.at[n, k, lap],
                device_id=(section, dp + 1 - 2 * core),
                device_id_type=MESH,
            )
            for n, (src, dst) in enumerate(((hs, hx), (ub, ux)))
        ]

    def await_bytes(ref, sem):
        pltpu.make_async_copy(ref, ref, sem).wait()

    def plane_copy(lap, k, to):
        return pltpu.make_async_remote_copy(
            src_ref=pk[k].at[lap, to],
            dst_ref=rs[k].at[lap, chip],
            send_sem=plane_send.at[k, lap],
            recv_sem=plane_recv.at[k, lap],
            device_id=(section, to * 2 + core),
            device_id_type=MESH,
        )

    def weight_term(lap, k):
        def product(left, right):
            rows = batches * ROWS[k]
            return dot_tn(left[k][lap].reshape(rows, channels), right[k][lap].reshape(rows, -1))

        grads = product(hs, ub)
        await_bytes(hx[k].at[lap], pair_recv.at[0, k, lap])
        await_bytes(ux[k].at[lap], pair_recv.at[1, k, lap])
        grads = grads + product(hx, ux)
        for n in range(len(SLOTS[k])):
            dwf[n] = grads[:, channels * n : channels * (n + 1)]
        low = lax.broadcasted_iota(jnp.int32, (8, channels), 0) < 4

        def rows_of(n, start):
            return dwf[n, pl.ds(pl.multiple_of(start, 8), 8), :]

        def block(j):
            whole = [rows_of(n, 24 * j + 16 * core) for n in range(len(SLOTS[k]))]
            middle = [rows_of(n, 24 * j + 8) for n in range(len(SLOTS[k]))]
            raised = jnp.where(core == 0, middle[0], pltpu.roll(middle[0], 4, 0))
            if k == 2:
                return jnp.concatenate([whole[0], raised], 0).astype(BF16)
            lowered = jnp.where(core == 0, pltpu.roll(middle[1], 4, 0), middle[1])
            mixed = jnp.where(low, raised, lowered)
            last = jnp.concatenate([mixed[:, 256:], jnp.zeros((8, LANES), F32)], 1)
            side = jnp.concatenate([mixed[:, :256], last], 0)
            return jnp.concatenate([jnp.concatenate(whole, 0), side], 1).astype(BF16)

        def pack(off, carry):
            j = lax.rem(chip + off, chips)
            pk[k][lap, j] = block(j)
            plane_copy(lap, k, j).start()
            return carry

        lax.fori_loop(1, chips, pack, 0, unroll=min(5, chips - 1))
        rs[k][lap, chip] = block(chip)

    def collect(lap, k):
        await_bytes(rs[k].at[lap, 0 : chips - 1], plane_recv.at[k, lap])
        total = rs[k][lap, 0].astype(F32)
        for j in range(1, chips):
            total = total + rs[k][lap, j].astype(F32)
        total = total * scale
        if k == 2:
            parts = [(0, total[0:8], total[8:12])]
        else:
            mixed = jnp.concatenate([total[0:8, channels:], total[8:16, channels : channels + LANES]], 1)
            parts = [
                (SLOTS[k][0], total[0:8, :channels], mixed[0:4]),
                (SLOTS[k][1], total[8:16, :channels], mixed[4:8]),
            ]
        for slot, whole, part in parts:

            @pl.when(core == 0)
            def _():
                for n in range(8):
                    wout[lap, slot, n] = whole[n : n + 1]
                for n in range(4):
                    wout[lap, slot, 8 + n] = part[n : n + 1]

            @pl.when(core == 1)
            def _():
                for n in range(4):
                    wout[lap, slot, n] = part[n : n + 1]
                for n in range(8):
                    wout[lap, slot, 4 + n] = whole[n : n + 1]

    fy[...] = jnp.zeros_like(fy)

    def prepare_range(lo, hi):
        def one(p, carry):
            prepare(p)
            return carry

        lax.fori_loop(lo, hi, one, 0)

    prepare_range(0, jnp.where(section == 3, 1, batches))

    def turn_rest():
        turn_weights(1, (3, 4, 0))
        inputs[7].wait()
        inputs[8].wait()
        turn_weights(0, range(5))

    @pl.when(section != 3)
    def _():
        turn_rest()

    inputs[6].wait()
    inputs[9].wait()
    pl.semaphore_wait(barrier, 4 + chips - 1)

    def run_lap(turn_index, carry):
        lap = 1 - turn_index

        def first(b, carry):
            now = jnp.where(section == 3, batches * turn_index + b, batches)
            until = jnp.where(section == 3, now + 1, batches + batches)
            late = (section == 3) & (lap == 1) & (b >= 1)
            fill = (section == 3) & (lap == 0) & (b == 0)
            early = (section != 3) & (lap == 1) & (b == 0)
            fill = fill | early
            lo = jnp.where(fill, batches, now)
            hi = jnp.where(fill, 2 * batches, jnp.where(late, until, lo))
            prepare_range(lo, hi)
            unit(lap, b, 0)
            unit(lap, b, 1)
            return carry

        lax.fori_loop(0, batches, first, 0)

        @pl.when((section == 3) & (lap == 1))
        def _():
            turn_rest()

        now = (section != 3) | (lap == 0)
        soon = jnp.where((section == 0) & (lap == 0), 0, 1)

        def second(b, carry):
            unit(lap, b, 2)
            unit(lap, b, 3)

            @pl.when((b == soon) & now)
            def _():
                weight_term(lap, 0)

            return carry

        lax.fori_loop(0, batches, second, 0)

        def third(b, carry):
            unit(lap, b, 4)
            unit(lap, b, 5)

            @pl.when((section == 0) & (lap == 0) & (b < batches - 1))
            def _():
                finish(b)

            @pl.when((b == soon) & now)
            def _():
                weight_term(lap, 1)

            return carry

        lax.fori_loop(0, batches, third, 0)

        @pl.when(now)
        def _():
            weight_term(lap, 2)

        @pl.when((section == 0) & (lap == 0))
        def _():
            finish(batches - 1)

        return carry

    lax.fori_loop(0, 2, run_lap, 0)

    @pl.when(section == 3)
    def _():
        for k in range(3):
            weight_term(1, k)

    for lap, k in ((1, 0), (1, 1), (1, 2), (0, 0), (0, 1)):
        collect(lap, k)


    @pl.when(section == 0)
    def _():
        for b in range(batches):
            deliver(b, fb[b, 0])
        await_bytes(fb.at[0:3], fin_send.at[0])

    await_bytes(ob.at[1], ring_send.at[1])

    @pl.when(section != 0)
    def _():
        await_bytes(ob.at[0], ring_send.at[0])

    for lap in (1, 0):
        for k in range(3):
            await_bytes(hs[k].at[lap], pair_send.at[0, k, lap])
            await_bytes(ub[k].at[lap], pair_send.at[1, k, lap])
            await_bytes(pk[k].at[lap, 0 : chips - 1], plane_send.at[k, lap])

    collect(0, 2)

    @pl.when(section != 0)
    def _():
        for b in range(batches):
            final_copy(b, section).wait_recv()
            deliver(b, frx[b])


def body(n_dp, h_saved, out_cot, so2_weight, radial, edge_angle, edge_atoms, edge_count, atom_count):
    batches, atom_slots, coeff_rows, channels = out_cot.shape
    edges = edge_angle.shape[1]
    share = share_of(channels, n_dp)
    chips = n_dp // 2
    slots = 2 * batches
    scale = 1.0 / math.sqrt(n_dp * batches * edges)
    vmem = pl.BlockSpec(memory_space=pltpu.VMEM)
    dma = pltpu.SemaphoreType.DMA
    h = h_saved[:, 0].transpose(0, 1, 3, 2, 4)
    g0 = out_cot.transpose(0, 2, 1, 3)
    w = so2_weight[:, 0]
    args = (h, g0, w, radial, edge_angle, edge_atoms, edge_count, atom_count)
    homes = [pltpu.VMEM(a.shape, a.dtype) for a in args[:6]] + [pltpu.SMEM(a.shape, a.dtype) for a in args[6:]]
    in_grad, wout = pl.pallas_call(
        functools.partial(kernel, n_dp, scale),
        out_shape=(
            pltpu.VMEM((batches, coeff_rows, 2, channels), BF16),
            pltpu.VMEM((2, 5, share, 1, channels), F32),
        ),
        in_specs=[pl.BlockSpec(memory_space=pl.ANY)] * 8,
        out_specs=(vmem, vmem),
        scratch_shapes=homes
        + [
            pltpu.VMEM((2, 5 * channels, channels), BF16),
            pltpu.VMEM((2, 2 * batches, edges), F32),
            pltpu.VMEM((batches, 5, 8, 8, channels), F32),
            pltpu.VMEM((batches, 5, 8, 8, channels), F32),
        ]
        + [pltpu.VMEM((2, batches, r, channels), BF16) for r in ROWS]
        + [
            pltpu.VMEM((20, 8, channels), F32),
            pltpu.VMEM((2, batches, coeff_rows, 8, channels), F32),
            pltpu.VMEM((2, batches, 8, channels), F32),
            pltpu.VMEM((batches, 8, channels), F32),
            pltpu.VMEM((8, 8, channels), F32),
            pltpu.VMEM((2, batches, ROWS[0], 2 * channels), BF16),
            pltpu.VMEM((2, batches, ROWS[1], 2 * channels), BF16),
            pltpu.VMEM((2, batches, ROWS[2], channels), BF16),
        ]
        + [pltpu.VMEM((slots, r, channels), BF16) for r in UNIT_ROWS]
        + [
            pltpu.VMEM((2, batches * sum(UNIT_ROWS), channels), BF16),
            pltpu.VMEM((channels // LANES, 152, LANES), F32),
            pltpu.VMEM((channels // LANES, 48, LANES), F32),
            pltpu.VMEM((batches, 4, 48, channels), BF16),
            pltpu.VMEM((batches, 48, channels), BF16),
            pltpu.VMEM((2, channels, channels), F32),
        ]
        + [pltpu.VMEM((2, batches, r, channels), BF16) for r in ROWS]
        + [
            pltpu.VMEM((2, batches, ROWS[0], 2 * channels), BF16),
            pltpu.VMEM((2, batches, ROWS[1], 2 * channels), BF16),
            pltpu.VMEM((2, batches, ROWS[2], channels), BF16),
        ]
        + [pltpu.VMEM((2, chips, 16, n), BF16) for n in WIDE]
        + [pltpu.VMEM((2, chips, 16, n), BF16) for n in WIDE]
        + [
            dma((10,)),
            dma((2,)),
            dma((len(UNITS), slots)),
            dma((1,)),
            dma((batches,)),
            dma((2, 3, 2)),
            dma((2, 3, 2)),
            dma((3, 2)),
            dma((3, 2)),
        ],
        compiler_params=pltpu.CompilerParams(
            collective_id=0, has_side_effects=True, vmem_limit_bytes=60 * 1024 * 1024
        ),
        name="window_backward",
    )(*args)
    return in_grad.transpose(0, 2, 1, 3), wout.transpose(0, 3, 1, 2, 4)


def solution(mesh):
    placed = (
        P(None, "section", "dp", None, None, None),
        P("dp", None, None, None),
        P(None, "section", None, None, None),
        P("dp", None, None),
        P("dp", None),
        P("dp", None, None),
        P("dp"),
        P("dp"),
    )
    return jax.shard_map(
        functools.partial(body, mesh.shape["dp"]),
        mesh=mesh,
        in_specs=placed,
        out_specs=(P("dp", "section", None, None), P(None, "section", None, "dp", None)),
        check_vma=False,
    )
```
